128 devices in a mesh: row: 16 (over x, y), col: 8 (over z, core).
Axes of the slice: x: 4, y: 4, z: 4, core: 2. Of those that a mesh axis runs over, the one named last changes fastest.
Arguments:
- amplitudes: bfloat16 [4, 4608, 4608], P(None, 'row', 'col'), may hold values from -6 to 6
- integrals: bfloat16 [4, 4608, 4608], P(None, 'col', 'row'), may hold values from -0.09375 to 0.09375
- pair_energy: float32 [4, 4608], replicated, may hold values from 0.5 to 3
- block_len: int32 [4, 8], replicated, may hold values from 1 to 576, 4032 in all within a row
Outputs:
- update: float32 [4, 4608, 4608], P(None, ('row', 'col'))
The draws below stay inside these ranges and needn't reach their ends.
Inputs may be any that keep to these rules, and one draw needn't show every extreme that they name: `block_len`: each slice's block lengths sum to 4032; some block of every slice is full.
All inputs are finite; a program needn't handle non-finite values.
Results may differ from the reference program's by a relative error of at most 0.015.
Values may be sent and summed in bfloat16 or wider, within the bound.
A program may use at most 128 MiB of HBM per device.

```python
import math
import jax
import jax.numpy as jnp
import numpy as np

NPAIR = 4608
IRREPS = 8
SLICES = 4
CAP = 576
N_COL = 8


def spiked(drawn, stream_key, source, target, parts, factor):
    def block_of(dim):
        return (jnp.arange(drawn.shape[dim]) // (drawn.shape[dim] // parts)).reshape((-1,) + (1,) * (drawn.ndim - 1 - dim))

    one_side = jax.random.permutation(stream_key, parts)[block_of(target)]
    other_side = (block_of(target) + parts // 2) % parts
    return jnp.where((block_of(source) == one_side) | (block_of(source) == other_side), factor * drawn, drawn)


def steps_of(rng, dims, split, smallest, largest):
    level = 1.0
    for dim, blocks in split:
        draws = jax.random.uniform(jax.random.fold_in(jax.random.fold_in(rng, 6), dim), (blocks,), jnp.float32, smallest / len(split), largest / len(split))
        level = level * jnp.repeat(jnp.exp(draws), dims[dim] // blocks).reshape((-1,) + (1,) * (len(dims) - 1 - dim))
    return level


def length_profile(amount, total, bound, skew):
    loads = [(1 << 20) // math.isqrt(standing ** skew) + 1 for standing in range(2, amount + 1)]
    rest, counts = total - bound - (amount - 1), [1] * (amount - 1)
    while rest > 0:
        candidates = [i for i in range(amount - 1) if counts[i] < bound]
        whole, remaining = sum([loads[i] for i in candidates]), rest
        for i in candidates:
            extra = min(bound - counts[i], max(1, remaining * loads[i] // whole), rest)
            counts[i] = counts[i] + extra
            rest = rest - extra
    return np.array([bound] + counts)


def ragged_sizes(rng, amount, total, bound, skew):
    if amount == 2:
        one = jax.random.randint(rng, (), max(1, total - bound), min(bound, total - 1) + 1)
        return jnp.stack([one, total - one])
    sizes = jnp.asarray(length_profile(amount, total, bound, skew), jnp.int32)
    couples = (amount - 1) // 2
    donor, sink = sizes[1:1 + 2 * couples:2], sizes[2:2 + 2 * couples:2]
    room = jnp.minimum(donor - 1, bound - sink)
    shifted = jax.random.randint(jax.random.fold_in(rng, 1), (couples,), 0, 1 << 20) % (room + 1)
    sizes = sizes.at[1:1 + 2 * couples:2].set(donor - shifted).at[2:2 + 2 * couples:2].set(sink + shifted)
    return sizes[jax.random.permutation(jax.random.fold_in(rng, 2), amount)]


def noise(key, shape, scale, reach, cuts=(), kind=jnp.bfloat16):
    entries = jax.random.normal(key, shape, jnp.float32) * scale
    if len(cuts) > 0:
        entries = steps_of(key, shape, cuts, -0.22, 0.18) * entries
    return jnp.clip(entries, min=-reach, max=reach).astype(kind)


def bell_draw_with(stream_key, dims, deviation, limit, split, heavy, kind=jnp.bfloat16):
    values = deviation * jax.random.normal(stream_key, dims, jnp.float32)
    if split:
        values = values * steps_of(stream_key, dims, split, -0.22, 0.18)
    return jnp.clip(spiked(values, jax.random.fold_in(stream_key, 3), *heavy), -limit, limit).astype(kind)


def setup_inputs(seed: int = 0) -> dict:
    key_of = jax.random.split(jax.random.key(seed), 5)
    amplitudes = bell_draw_with(key_of[0], (SLICES, NPAIR, NPAIR), 1.0, 6.0, ((1, 16), (2, 8)), (2, 1, 16, 2.0))
    integrals = noise(key_of[1], (SLICES, NPAIR, NPAIR), NPAIR ** -0.5, 0.09375, ((1, 8), (2, 16)))
    pair_energy = jnp.clip(jnp.exp(jax.random.uniform(key_of[2], (SLICES, NPAIR), jnp.float32, math.log(0.5), math.log(3.0))), 0.5, 3.0)
    block_len = jax.vmap(lambda own: ragged_sizes(own, IRREPS, 7 * CAP, CAP, 2))(jax.random.split(key_of[3], SLICES)).reshape((SLICES, IRREPS)).astype(jnp.int32)
    return dict(amplitudes=amplitudes, integrals=integrals, pair_energy=pair_energy, block_len=block_len)


def pair_live(lengths):
    capacity = NPAIR // IRREPS
    position = jnp.arange(NPAIR, dtype=jnp.int32)
    irrep_of = position // capacity
    onehot = (irrep_of[:, None] == jnp.arange(IRREPS, dtype=jnp.int32)[None, :]).astype(jnp.int32)
    limits = jnp.sum(onehot * lengths[None, :], axis=1)
    return ((position % capacity) < limits).astype(jnp.float32)


def reference(amplitudes, integrals, pair_energy, block_len):
    width = NPAIR // N_COL
    results = []
    for which in range(SLICES):
        live = pair_live(block_len[which])
        masked = amplitudes[which] * live.astype(jnp.bfloat16)[None, :]
        total = jnp.zeros((NPAIR, NPAIR), jnp.float32)
        for part in range(N_COL):
            left = masked[:, part * width:(part + 1) * width]
            right = integrals[which][part * width:(part + 1) * width, :]
            partial_value = jnp.dot(left, right, preferred_element_type=jnp.float32).astype(jnp.bfloat16)
            total = total + partial_value.astype(jnp.float32)
        cycle = total.astype(jnp.bfloat16).astype(jnp.float32)
        energy = pair_energy[which]
        update = live[:, None] * live[None, :] * (cycle + cycle.T) / (energy[:, None] + energy[None, :])
        results.append(update)
    return jnp.stack(results)
```

```python
import functools

import jax
import jax.numpy as jnp
from jax import lax
from jax.experimental import pallas as pl
from jax.experimental.pallas import tpu as pltpu
from jax.sharding import PartitionSpec as P

MESH = pl.DeviceIdType.MESH
BF = jnp.bfloat16
F32 = jnp.float32
I32 = jnp.int32


def nt(a, b):
    return lax.dot_general(a, b, (((1,), (1,)), ((), ())), preferred_element_type=F32)


def nn(a, b):
    return jnp.dot(a, b, preferred_element_type=F32)


def iota(shape, dim):
    return lax.broadcasted_iota(I32, shape, dim)


def natural(j):
    return 2 * (j & 3) + (j >> 2)


def kernel(
    a_hbm, b_hbm, e_ref, l_ref, o_hbm,
    av, bv, ga, gb, rg, ps, cx, pf, q1, q2, z1a, z1b, z2, own, db, hh, txm, txr,
    um, ur, tm, tr, tt, pm, eye, qp, sel, s1, s2, mk, er, ob,
    lsem, g1s, g1r, g2s, g2r, cs, cr, z1s, z1r, z2s, z2r, hs, hr, xs, xr, ts, tsr, osem,
):
    row = lax.axis_index("row")
    col = lax.axis_index("col")
    x, y = row // 4, row % 4
    z, c = col // 2, col % 2
    jme = c * 4 + z

    def at(dx, dy, dz, dc):
        return ((x + dx) % 4 * 4 + (y + dy) % 4, (z + dz) % 4 * 2 + (c + dc) % 2)

    def remote(src, dst, ssem, rsem, where):
        return pltpu.make_async_remote_copy(
            src_ref=src, dst_ref=dst, send_sem=ssem, recv_sem=rsem, device_id=where, device_id_type=MESH
        )

    def load(s):
        return (
            pltpu.make_async_copy(a_hbm.at[s], av.at[s], lsem.at[s, 0]),
            pltpu.make_async_copy(b_hbm.at[s], bv.at[s], lsem.at[s, 1]),
        )

    for s in range(4):
        for cp in load(s):
            cp.start()

    def rows_of(v, size):
        return pl.ds(pl.multiple_of(v * size, size), size)

    def gather1(s):
        out = []
        for d, step in ((0, 1), (1, 3)):
            to_y, to_x = at(0, step, 0, 0), at(step, 0, 0, 0)
            main = ga.at[s, :, rows_of(y, 32), :]
            out.append(remote(main, main, g1s.at[s, d, 0], g1r.at[s, d, 0], to_y))
            rem = rg.at[s, y]
            out.append(remote(rem, rem, g1s.at[s, d, 1], g1r.at[s, d, 1], to_y))
            blk = gb.at[s, rows_of(x, 288), :]
            out.append(remote(blk, blk, g1s.at[s, d, 2], g1r.at[s, d, 2], to_x))
        return out

    def gather2(s):
        out = []
        for d, step in ((0, 1), (1, 3)):
            to_y, to_x = at(0, step, 0, 0), at(step, 0, 0, 0)
            ysrc, xsrc = (y + 4 - step) % 4, (x + 4 - step) % 4
            main = ga.at[s, pl.ds(4 * d, 4), rows_of(ysrc, 32), :]
            out.append(remote(main, main, g2s.at[s, d, 0], g2r.at[s, d, 0], to_y))
            rem = rg.at[s, ysrc, pl.ds(16 * d, 16), :]
            out.append(remote(rem, rem, g2s.at[s, d, 1], g2r.at[s, d, 1], to_y))
            blk = gb.at[s, pl.ds(pl.multiple_of(xsrc * 288 + 144 * d, 16), 144), :]
            out.append(remote(blk, blk, g2s.at[s, d, 2], g2r.at[s, d, 2], to_x))
        return out

    def swap(s):
        return [remote(ps.at[s], cx.at[s], cs.at[s], cr.at[s], at(0, 0, 0, 1))]

    def zstep1(s):
        return [
            remote(q1.at[s, pl.ds(0, 80), :], z1a.at[s], z1s.at[s, 0], z1r.at[s, 0], at(0, 0, 1, 0)),
            remote(q1.at[s, pl.ds(80, 64), :], z1b.at[s], z1s.at[s, 1], z1r.at[s, 1], at(0, 0, 3, 0)),
        ]

    def zstep2(s):
        return [
            remote(q2.at[s, d], z2.at[s, d], z2s.at[s, d], z2r.at[s, d], at(0, 0, step, 0))
            for d, step in ((0, 1), (1, 3))
        ]

    def here_copies(s):
        out = []
        for d in (1, 2, 3):
            to = at(0, d, 0, 0)
            out.append(remote(
                db.at[s, rows_of((y + d) % 4, 32), :], hh.at[s, y, pl.ds(0, 32), :],
                hs.at[s, d - 1, 0], hr.at[s, d - 1, 0], to,
            ))
            out.append(remote(
                db.at[s, pl.ds(128, 16), :], hh.at[s, y, pl.ds(32, 16), :],
                hs.at[s, d - 1, 1], hr.at[s, d - 1, 1], to,
            ))
        return out

    def turn_copies(s):
        out = []
        for d in (1, 2, 3):
            to = at(d, 0, 0, 0)
            lanes = pl.ds(pl.multiple_of((x + d) % 4 * 256, 256), 384)
            out.append(remote(
                db.at[s, pl.ds(0, 128), lanes], txm.at[s, rows_of(x, 128), :],
                xs.at[s, d - 1, 0], xr.at[s, d - 1, 0], to,
            ))
            out.append(remote(
                db.at[s, pl.ds(128, 16), lanes], txr.at[s, rows_of(x, 16), :],
                xs.at[s, d - 1, 1], xr.at[s, d - 1, 1], to,
            ))
        return out

    def last_copies(s):
        out = []
        for i in range(1, 8):
            dz, dc = i // 2, i % 2
            to = at(0, 0, dz, dc)
            jto = (c + dc) % 2 * 4 + (z + dz) % 4
            lanes = rows_of(jme, 128)
            out.append(remote(um.at[s, jto], tm.at[s, :, :, lanes], ts.at[s, i - 1, 0], tsr.at[s, i - 1, 0], to))
            out.append(remote(ur.at[s, jto], tr.at[s, :, lanes], ts.at[s, i - 1, 1], tsr.at[s, i - 1, 1], to))
        return out

    def result_copy(s):
        return pltpu.make_async_copy(ob.at[s], o_hbm.at[s], osem.at[s])

    def start(copies):
        for cp in copies:
            cp.start()

    def arrive(copies):
        for cp in copies:
            cp.wait_recv()

    def prepare(s):
        for cp in load(s):
            cp.wait()
        limit = l_ref[s, col]
        masked = jnp.where(iota((288, 576), 1) < limit, av[s].astype(F32), 0.0).astype(BF)
        turned = nn(pm[...], masked).astype(BF)
        ga[s, :, rows_of(y, 32), :] = turned[:256].reshape(8, 32, 576)
        rg[s, y] = turned[256:]
        gb[s, rows_of(x, 288), :] = nt(eye[...], bv[s]).astype(BF)

    def multiply(s):
        arrive(gather2(s))
        rest = nn(qp[...], rg[s].reshape(128, 576)).astype(BF)
        ga[s, :, 128:144, :] = rest.reshape(8, 16, 576)

        def other(n, _):
            cols = pl.ds(pl.multiple_of(n * 384, 384), 384)
            lhs = ga[s, pl.ds((1 - c) * 4, 4)].reshape(576, 576)
            ps[s, :, :, cols] = nt(lhs, gb[s, cols, :]).astype(BF).reshape(4, 144, 384)
            return 0

        lax.fori_loop(0, 3, other, 0)
        start(swap(s))

        def mine(n, _):
            cols = pl.ds(pl.multiple_of(n * 384, 384), 384)
            lhs = ga[s, pl.ds(c * 4, 4)].reshape(576, 576)
            pf[:, :, cols] = nt(lhs, gb[s, cols, :]).reshape(4, 144, 384)
            return 0

        lax.fori_loop(0, 3, mine, 0)

    def first_sum(s):
        arrive(swap(s))
        far = (z + 2) % 4

        def add(i, _):
            rows = rows_of(i, 16)
            q1[s, rows, :] = (pf[far, rows, :] + cx[s, far, rows, :].astype(F32)).astype(BF)
            return 0

        lax.fori_loop(0, 9, add, 0)
        start(zstep1(s))

    def second_sum(s):
        arrive(zstep1(s))
        up, down = (z + 1) % 4, (z + 3) % 4

        def add_low(i, _):
            rows = rows_of(i, 16)
            q2[s, 0, rows, :] = (
                pf[up, rows, :] + cx[s, up, rows, :].astype(F32) + z1a[s, rows, :].astype(F32)
            ).astype(BF)
            q2[s, 1, rows, :] = (pf[down, rows, :] + cx[s, down, rows, :].astype(F32)).astype(BF)
            return 0

        lax.fori_loop(0, 5, add_low, 0)

        def add_high(i, _):
            rows = pl.ds(pl.multiple_of(i * 16 + 80, 16), 16)
            got = rows_of(i, 16)
            q2[s, 0, rows, :] = (pf[up, rows, :] + cx[s, up, rows, :].astype(F32)).astype(BF)
            q2[s, 1, rows, :] = (
                pf[down, rows, :] + cx[s, down, rows, :].astype(F32) + z1b[s, got, :].astype(F32)
            ).astype(BF)
            return 0

        lax.fori_loop(0, 4, add_high, 0)
        start(zstep2(s))

        def keep(i, _):
            rows = rows_of(i, 16)
            own[rows, :] = pf[z, rows, :] + cx[s, z, rows, :].astype(F32)
            return 0

        lax.fori_loop(0, 9, keep, 0)

    def whole_sum(s):
        arrive(zstep2(s))

        def add(i, _):
            rows = rows_of(i, 16)
            db[s, rows, :] = (own[rows, :] + z2[s, 0, rows, :].astype(F32) + z2[s, 1, rows, :].astype(F32)).astype(BF)
            return 0

        lax.fori_loop(0, 9, add, 0)
        start(turn_copies(s))
        start(here_copies(s))
        hh[s, y, 0:32, :] = db[s, rows_of(y, 32), :]
        hh[s, y, 32:48, :] = db[s, 128:144, :]
        lanes = pl.ds(pl.multiple_of(x * 256, 256), 384)
        txm[s, rows_of(x, 128), :] = db[s, 0:128, lanes]
        txr[s, rows_of(x, 16), :] = db[s, 128:144, lanes]

    def turn(s):
        arrive(turn_copies(s))
        main = nt(sel[...], txm[s]).astype(BF)
        for xx in range(4):
            um[s, :, xx] = main[:, 128 * xx:128 * xx + 128].reshape(8, 48, 128)
        rest = nt(sel[...], txr[s])
        rest = jnp.concatenate([rest, jnp.zeros_like(rest)], axis=1)
        ur[s] = rest.astype(BF).reshape(8, 48, 128)
        start(last_copies(s))
        lanes = rows_of(jme, 128)
        tm[s, :, :, lanes] = um[s, jme]
        tr[s, :, lanes] = ur[s, jme]

    def finish(s):
        arrive(last_copies(s))
        lhs = tm[s].reshape(192, 1024)
        rest = tr[s]
        rest = jnp.concatenate([rest * mk[16 * xx:16 * xx + 1, :] for xx in range(4)], axis=0)
        for n in range(3):
            cols = slice(384 * n, 384 * n + 384)
            tt[:, :, cols] = (nn(lhs, s1[:, cols]) + nn(rest, s2[:, cols])).reshape(4, 48, 384)
        arrive(here_copies(s))
        dev = row * 8 + col
        row_limit = l_ref[s, dev // 16] - (dev % 16) * 36
        row_live = (iota((36, 1), 0) < row_limit).astype(F32)
        row_energy = er[s, 0:36, 0:1]
        pieces = []
        for yy in range(4):
            part = hh[s, yy].astype(F32)
            low = pltpu.roll(part[32:48], (16 - 4 * y) % 16, 0)
            pieces.append(jnp.concatenate([part[:32], low[:8]], axis=0))
        lane = iota((1, 1152), 1)
        for xx in range(4):
            local = jnp.concatenate([p[:, 288 * xx:288 * xx + 288] for p in pieces], axis=1)
            total = local[:36] + tt[xx, 0:36, :]
            bound = jnp.where(lane < 576, l_ref[s, 2 * xx], l_ref[s, 2 * xx + 1] + 576)
            col_live = (lane < bound).astype(F32)
            energy = row_energy + e_ref[pl.ds(s, 1), 1152 * xx:1152 * xx + 1152]
            ob[s, :, 1152 * xx:1152 * xx + 1152] = row_live * col_live * total / energy
        result_copy(s).start()

    def early_constants():
        i = iota((288, 288), 0)
        k = iota((288, 288), 1)
        head = 36 * natural(i >> 5) + (i & 31)
        tail = 36 * natural((i - 256) >> 2) + 32 + (i & 3)
        pm[...] = (k == jnp.where(i < 256, head, tail)).astype(F32).astype(BF)
        eye[...] = (k == i).astype(F32).astype(BF)
        i = iota((128, 128), 0)
        k = iota((128, 128), 1)
        qp[...] = (k == 32 * ((i >> 2) & 3) + 4 * (i >> 4) + (i & 3)).astype(F32).astype(BF)

    def late_constants():
        j, t, k = (iota((8, 48, 384), n) for n in range(3))
        hit = (k == 32 * x + 36 * natural(j) + t) & (t < 36)
        sel[...] = hit.astype(F32).astype(BF).reshape(384, 384)

        def fill(j, _):
            rows = rows_of(j, 128)
            r = iota((128, 1152), 0)
            k = iota((128, 1152), 1)
            base = 36 * natural(j)
            s1[rows, :] = (k == 288 * (r >> 5) + base + (r & 31)).astype(F32).astype(BF)
            hit = (k == 288 * ((r >> 2) & 3) + base + 32 + (r & 3)) & (r < 64)
            s2[rows, :] = hit.astype(F32).astype(BF)
            return 0

        lax.fori_loop(0, 8, fill, 0)
        r = iota((64, 1024), 0)
        k = iota((64, 1024), 1)
        mk[...] = (((k & 127) >> 4) == (r >> 4)).astype(F32).astype(BF)
        dev = row * 8 + col
        pick = iota((40, 4608), 1) == iota((40, 4608), 0) + dev * 36
        for s in range(4):
            got = jnp.sum(jnp.where(pick, e_ref[s:s + 1, :], 0.0), axis=1, keepdims=True)
            er[s] = jnp.broadcast_to(got, (40, 128))

    early_constants()
    prepare(0)
    barrier = pltpu.get_barrier_semaphore()
    partners = [at(d, 0, 0, 0) for d in (1, 2, 3)] + [at(0, d, 0, 0) for d in (1, 2, 3)]
    partners += [at(0, 0, i // 2, i % 2) for i in range(1, 8)]
    for p in partners:
        pl.semaphore_signal(barrier, 1, device_id=p, device_id_type=MESH)
    pl.semaphore_wait(barrier, len(partners))
    start(gather1(0))
    late_constants()

    def during(r, low, high, what):
        @pl.when((r >= low) & (r < high))
        def _():
            what(r - low)

    def forward(s):
        arrive(gather1(s))
        start(gather2(s))

    def one_round(r, _):
        during(r, 0, 3, lambda s: prepare(s + 1))
        during(r, 0, 4, forward)
        during(r, 0, 3, lambda s: start(gather1(s + 1)))
        during(r, 1, 5, second_sum)
        during(r, 2, 6, turn)
        during(r, 0, 4, multiply)
        during(r, 0, 4, first_sum)
        during(r, 1, 5, whole_sum)
        during(r, 2, 6, finish)
        return 0

    lax.fori_loop(0, 6, one_round, 0)

    def drain(s, _):
        for copies in (gather1, gather2, swap, zstep1, zstep2, here_copies, turn_copies, last_copies):
            for cp in copies(s):
                cp.wait_send()
        result_copy(s).wait()
        return 0

    lax.fori_loop(0, 4, drain, 0)


def body(amplitudes, integrals, pair_energy, block_len):
    bf = lambda *shape: pltpu.VMEM(shape, BF)
    f32 = lambda *shape: pltpu.VMEM(shape, F32)
    dma = lambda *shape: pltpu.SemaphoreType.DMA(shape)
    scratch = [
        bf(4, 288, 576), bf(4, 576, 288),
        bf(4, 8, 144, 576), bf(4, 1152, 576), bf(4, 4, 32, 576),
        bf(4, 4, 144, 1152), bf(4, 4, 144, 1152), f32(4, 144, 1152),
        bf(4, 144, 1152), bf(4, 2, 144, 1152),
        bf(4, 80, 1152), bf(4, 64, 1152), bf(4, 2, 144, 1152),
        f32(144, 1152), bf(4, 144, 1152),
        bf(4, 4, 48, 1152), bf(4, 512, 384), bf(4, 64, 384),
        bf(4, 8, 4, 48, 128), bf(4, 8, 48, 128), bf(4, 4, 48, 1024), bf(4, 48, 1024),
        f32(4, 48, 1152),
        bf(288, 288), bf(288, 288), bf(128, 128), bf(384, 384), bf(1024, 1152), bf(1024, 1152), bf(64, 1024),
        f32(4, 40, 128), f32(4, 36, 4608),
        dma(4, 2), dma(4, 2, 3), dma(4, 2, 3), dma(4, 2, 3), dma(4, 2, 3), dma(4), dma(4),
        dma(4, 2), dma(4, 2), dma(4, 2), dma(4, 2),
        dma(4, 3, 2), dma(4, 3, 2), dma(4, 3, 2), dma(4, 3, 2), dma(4, 7, 2), dma(4, 7, 2), dma(4),
    ]
    count, npairs = pair_energy.shape
    return pl.pallas_call(
        kernel,
        out_shape=jax.ShapeDtypeStruct((count, npairs // 128, npairs), F32),
        in_specs=[
            pl.BlockSpec(memory_space=pl.ANY),
            pl.BlockSpec(memory_space=pl.ANY),
            pl.BlockSpec(memory_space=pltpu.VMEM),
            pl.BlockSpec(memory_space=pltpu.SMEM),
        ],
        out_specs=pl.BlockSpec(memory_space=pl.ANY),
        scratch_shapes=scratch,
        compiler_params=pltpu.CompilerParams(
            collective_id=0, has_side_effects=True, vmem_limit_bytes=63 << 20
        ),
        name="cycle",
    )(amplitudes, integrals, pair_energy, block_len)


def solution(mesh):
    return jax.shard_map(
        body,
        mesh=mesh,
        in_specs=(P(None, "row", "col"), P(None, "col", "row"), P(), P()),
        out_specs=P(None, ("row", "col"), None),
        check_vma=False,
    )
```

```python
import functools

import jax
import jax.numpy as jnp
from jax import lax
from jax.experimental import pallas as pl
from jax.experimental.pallas import tpu as pltpu
from jax.sharding import PartitionSpec as P

MESH = pl.DeviceIdType.MESH
BF = jnp.bfloat16
F32 = jnp.float32
I32 = jnp.int32

PARTS = ((0, 80, 48), (80, 64, 32))
PIECES = ((0, 656), (656, 640))

ORDER = (
    ("ready", 1), ("ready", 2), ("relay", 0), ("mul0", 0), ("mul1", 0), ("far0", 0), ("ready", 3), ("relay", 1),
    ("far1", 0), ("near0", 0), ("near1", 0), ("mul0", 1), ("mul1", 1), ("far0", 1), ("relay", 2), ("far1", 1),
    ("near0", 1), ("near1", 1), ("mul0", 2), ("mul1", 2), ("relay", 3), ("sum0", 1), ("far0", 2), ("sum0", 0),
    ("far1", 2), ("near0", 2), ("sum1", 1), ("near1", 2), ("sum1", 0), ("mul0", 3), ("mul1", 3), ("far0", 3),
    ("far1", 3), ("turn", 0), ("near0", 3), ("near1", 3), ("sum0", 2), ("sum1", 2), ("turn", 2), ("sum0", 3),
    ("turn", 1), ("sum1", 3), ("done", 2), ("turn", 3), ("done", 0), ("done", 1), ("done", 3),
)


def nt(a, b):
    return lax.dot_general(a, b, (((1,), (1,)), ((), ())), preferred_element_type=F32)


def nn(a, b):
    return jnp.dot(a, b, preferred_element_type=F32)


def iota(shape, dim):
    return lax.broadcasted_iota(I32, shape, dim)


def natural(j):
    return 2 * (j & 3) + (j >> 2)


def ones_where(hit):
    return hit.astype(F32).astype(BF)


def kernel(
    a_hbm, b_hbm, e_ref, l_ref, o_hbm,
    av, bv, ra, rb, rhs, grem, gremf, lhs, ps, cx, pf, q1, q2, z1, z2, own, db, dx, hm, ht, hr, txm, txs, txr,
    wm, wr, um, tm, tt, pm, qp, ue, fold, sel_m, sel_x, sel_a, s1, s2, mk, er, ob,
    lsem, gos, gor, grs, grr, cs, cr, z1s, z1r, z2s, z2r, hs, hrr, xs, xr, ts, tsr, osem,
):
    row = lax.axis_index("row")
    col = lax.axis_index("col")
    x, y = row // 4, row % 4
    z, c = col // 2, col % 2
    jme = c * 4 + z

    def at(dx, dy, dz, dc):
        return ((x + dx) % 4 * 4 + (y + dy) % 4, (z + dz) % 4 * 2 + (c + dc) % 2)

    def remote(src, dst, ssem, rsem, where):
        return pltpu.make_async_remote_copy(
            src_ref=src, dst_ref=dst, send_sem=ssem, recv_sem=rsem, device_id=where, device_id_type=MESH
        )

    def load(s):
        return (
            pltpu.make_async_copy(a_hbm.at[s], av.at[s], lsem.at[s, 0]),
            pltpu.make_async_copy(b_hbm.at[s], bv.at[s], lsem.at[s, 1]),
        )

    for s in range(4):
        for cp in load(s):
            cp.start()

    def rows_of(v, size):
        return pl.ds(pl.multiple_of(v * size, size), size)

    def gather_own(s, which):
        out = []
        for d, step in ((0, 1), (1, 3)):
            first, size = PIECES[d ^ which]
            rows = pl.ds(first, size)
            blk = ra.at[s, y, rows, :]
            out.append(remote(blk, blk, gos.at[s, d, which, 0], gor.at[s, d, which, 0], at(0, step, 0, 0)))
            blk = rb.at[s, x, rows, :]
            out.append(remote(blk, blk, gos.at[s, d, which, 1], gor.at[s, d, which, 1], at(step, 0, 0, 0)))
        return out

    def gather_relay(s):
        out = []
        for d, step in ((0, 1), (1, 3)):
            first, size = PIECES[d]
            rows = pl.ds(first, size)
            blk = ra.at[s, (y + 4 - step) % 4, rows, :]
            out.append(remote(blk, blk, grs.at[s, d, 0], grr.at[s, d, 0], at(0, step, 0, 0)))
            blk = rb.at[s, (x + 4 - step) % 4, rows, :]
            out.append(remote(blk, blk, grs.at[s, d, 1], grr.at[s, d, 1], at(step, 0, 0, 0)))
        return out

    def swap(s, p):
        rows = pl.ds(*PARTS[p][:2])
        return [remote(ps.at[s, :, rows, :], cx.at[s, :, rows, :], cs.at[s, p], cr.at[s, p], at(0, 0, 0, 1))]

    def zstep1(s, p):
        first, size, up = PARTS[p]
        out = []
        for d, step, rows in ((0, 1, pl.ds(first, up)), (1, 3, pl.ds(first + up, size - up))):
            out.append(remote(
                q1.at[s, rows, :], z1.at[s, rows, :], z1s.at[s, p, d], z1r.at[s, p, d], at(0, 0, step, 0)
            ))
        return out

    def zstep2(s, p):
        rows = pl.ds(*PARTS[p][:2])
        return [
            remote(q2.at[s, d, rows, :], z2.at[s, d, rows, :], z2s.at[s, p, d], z2r.at[s, p, d], at(0, 0, step, 0))
            for d, step in ((0, 1), (1, 3))
        ]

    def here_copies(s):
        out = []
        for d in (1, 2, 3):
            to, yto = at(0, d, 0, 0), (y + d) % 4
            out.append(remote(
                db.at[s, rows_of(yto, 32), :], hm.at[s, y], hs.at[s, d - 1, 0], hrr.at[s, d - 1, 0], to
            ))
            out.append(remote(ht.at[s, yto], hr.at[s, y], hs.at[s, d - 1, 1], hrr.at[s, d - 1, 1], to))
        return out

    def turn_copies(s, p):
        out = []
        for d in (1, 2, 3):
            to, xto = at(d, 0, 0, 0), (x + d) % 4
            if p == 2:
                out.append(remote(txs.at[s, xto], txr.at[s, x], xs.at[s, d - 1, p], xr.at[s, d - 1, p], to))
            else:
                rows = pl.ds(*PARTS[p][:2])
                out.append(remote(
                    dx.at[s, xto, rows, :], txm.at[s, x, rows, :],
                    xs.at[s, d - 1, p], xr.at[s, d - 1, p], to,
                ))
        return out

    def last_copies(s):
        out = []
        for i in (2, 6, 4, 3, 7, 5, 1):
            dz, dc = i // 2, i % 2
            jto = (c + dc) % 2 * 4 + (z + dz) % 4
            out.append(remote(
                um.at[s, jto], tm.at[s, jme], ts.at[s, i - 1], tsr.at[s, i - 1], at(0, 0, dz, dc)
            ))
        return out

    def result_copy(s):
        return pltpu.make_async_copy(ob.at[s], o_hbm.at[:, s, :], osem.at[s])

    def start(copies):
        for cp in copies:
            cp.start()

    def arrive(copies):
        for cp in copies:
            cp.wait_recv()

    def fold_lanes(low, high):
        return jnp.concatenate([low, high], axis=1)

    def ready(s):
        for cp in load(s):
            cp.wait()
        limit = l_ref[s, col]
        masked = jnp.where(iota((288, 576), 1) < limit, av[s].astype(F32), 0.0).astype(BF)
        turned = nn(pm[...], masked)
        b = bv[s]
        for k in range(4):
            ra[s, y, 288 * k:288 * k + 288, :] = turned[:, 128 * k:128 * k + 128].astype(BF)
            rb[s, x, 288 * k:288 * k + 288, :] = b[:, 128 * k:128 * k + 128]
        rest = turned[:, 512:576]
        ra[s, y, 1152:1280, :] = fold_lanes(rest[0:128], rest[128:256]).astype(BF)
        ra[s, y, 1280:1296, :] = fold_lanes(rest[256:272], rest[272:288]).astype(BF)
        rest = b[:, 512:576].astype(F32)
        rb[s, x, 1152:1296, :] = fold_lanes(rest[0:144], rest[144:288]).astype(BF)

    def relay(s):
        arrive(gather_own(s, 0))
        start(gather_relay(s))

        @pl.when(s < 3)
        def _():
            start(gather_own(s + 1, 0))
            start(gather_own(s + 1, 1))

    def unfold(s):
        got = nn(rb[s, :, 1152:1296, :].reshape(576, 128), ue[...]).astype(BF)
        for xx in range(4):
            for k in range(4):
                lanes = slice(128 * k, 128 * k + 128)
                rhs[256 * xx:256 * xx + 256, lanes] = rb[s, xx, 288 * k:288 * k + 256, :]
                rhs[1024 + 32 * xx:1056 + 32 * xx, lanes] = rb[s, xx, 288 * k + 256:288 * k + 288, :]
            low, high = got[144 * xx:144 * xx + 144, 0:256], got[144 * xx:144 * xx + 144, 256:512]
            rhs[256 * xx:256 * xx + 144, 512:768] = low
            rhs[256 * xx + 144:256 * xx + 256, 512:768] = high[0:112]
            rhs[1024 + 32 * xx:1056 + 32 * xx, 512:768] = high[112:144]
        for k in range(4):
            grem[:, 128 * k:128 * k + 128] = nn(
                qp[...], ra[s, :, 288 * k + 256:288 * k + 288, :].reshape(128, 128)
            ).astype(BF)
        gremf[...] = nn(fold[...], ra[s, :, 1280:1296, :].reshape(64, 128)).astype(BF)

    def gather_lhs(s, p, h):
        first, size, _ = PARTS[p]
        lanes = pl.ds(pl.multiple_of(512 + 128 * h, 128), 128)
        lhs[:, pl.ds(pl.multiple_of(640 - 128 * h, 128), 128)] = jnp.zeros((320, 128), BF)
        for zz in range(4):
            at_row = size * zz
            j = h * 4 + zz
            spans = ((0, 0, 32), (1, 0, 32), (2, 0, 16)) if p == 0 else ((2, 16, 16), (3, 0, 32))
            for yy, skip, n in spans:
                for k in range(4):
                    rows = pl.ds(pl.multiple_of(288 * k + 32 * j + skip, 16), n)
                    lhs[at_row:at_row + n, 128 * k:128 * k + 128] = ra[s, yy, rows, :]
                lhs[at_row:at_row + n, lanes] = ra[s, yy, 1152 + 32 * zz + skip:1152 + 32 * zz + skip + n, :]
                at_row += n
            if p == 1:
                lhs[at_row:at_row + 16, 0:512] = grem[rows_of(j, 16), :]
                lhs[at_row:at_row + 16, lanes] = gremf[16 * zz:16 * zz + 16, :]

    def multiply(p, s):
        if p == 0:
            arrive(gather_own(s, 1))
            arrive(gather_relay(s))
            unfold(s)
        first, size, _ = PARTS[p]
        rows = slice(first, first + size)

        def product(h):
            gather_lhs(s, p, h)
            return nt(lhs[0:4 * size, :], rhs[...]).reshape(4, size, 1152)

        ps[s, :, rows, :] = product(1 - c).astype(BF)
        start(swap(s, p))
        pf[:, rows, :] = product(c)

    def each16(first, count, what):
        def one(i, _):
            what(pl.ds(pl.multiple_of(first + i * 16, 16), 16))
            return 0

        lax.fori_loop(0, count // 16, one, 0)

    def here_sum(s, zz, rows):
        return pf[zz, rows, :] + cx[s, zz, rows, :].astype(F32)

    def far(p, s):
        first, size, _ = PARTS[p]
        arrive(swap(s, p))

        def add(rows):
            q1[s, rows, :] = here_sum(s, (z + 2) % 4, rows).astype(BF)

        each16(first, size, add)
        start(zstep1(s, p))

    def near(p, s):
        first, size, up = PARTS[p]
        arrive(zstep1(s, p))
        zup, zdown = (z + 1) % 4, (z + 3) % 4

        def add_up(rows):
            q2[s, 0, rows, :] = (here_sum(s, zup, rows) + z1[s, rows, :].astype(F32)).astype(BF)
            q2[s, 1, rows, :] = here_sum(s, zdown, rows).astype(BF)

        def add_down(rows):
            q2[s, 0, rows, :] = here_sum(s, zup, rows).astype(BF)
            q2[s, 1, rows, :] = (here_sum(s, zdown, rows) + z1[s, rows, :].astype(F32)).astype(BF)

        each16(first, up, add_up)
        each16(first + up, size - up, add_down)
        start(zstep2(s, p))

        def keep(rows):
            own[s, rows, :] = here_sum(s, z, rows)

        each16(first, size, keep)

    def total(p, s):
        first, size, _ = PARTS[p]
        arrive(zstep2(s, p))

        def add(rows):
            v = own[s, rows, :] + z2[s, 0, rows, :].astype(F32) + z2[s, 1, rows, :].astype(F32)
            v = v.astype(BF)
            db[s, rows, :] = v
            for xx in range(4):
                dx[s, xx, rows, :] = v[:, 256 * xx:256 * xx + 256]

        each16(first, size, add)
        start(turn_copies(s, p))
        span = slice(first, first + size)
        txm[s, x, span, :] = dx[s, x, span, :]
        if p == 1:
            tail = db[s, :, 1024:1152].astype(F32)
            for xx in range(4):
                lanes = slice(32 * xx, 32 * xx + 32)
                packed = [tail[48 * g:48 * g + 48, lanes] for g in range(3)]
                packed.append(jnp.zeros((48, 32), F32))
                txs[s, xx] = jnp.concatenate(packed, axis=1).astype(BF)
            start(turn_copies(s, 2))
            txr[s, x] = txs[s, x]
            low = db[s, 128:144, :].astype(F32)
            for yy in range(4):
                mine = low[4 * yy:4 * yy + 4]
                ht[s, yy, :, 0:256] = jnp.concatenate(
                    [mine[:, 256 * xx:256 * xx + 256] for xx in range(4)], axis=0
                ).astype(BF)
                ht[s, yy, :, 256:384] = jnp.concatenate([mine[:, 1024:1152]] * 4, axis=0).astype(BF)
            start(here_copies(s))
            hm[s, y] = db[s, rows_of(y, 32), :]
            hr[s, y] = ht[s, y]

    def turn(s):
        for p in range(3):
            arrive(turn_copies(s, p))
        for xx in range(4):
            packed = txr[s, xx]
            groups = [packed * mk[8 + g:9 + g, 0:128] for g in range(3)]
            wm[128 * xx:128 * xx + 128, 0:256] = txm[s, xx, 0:128, :]
            wm[128 * xx:128 * xx + 48, 256:384] = groups[0]
            wm[128 * xx + 48:128 * xx + 96, 256:384] = groups[1]
            wm[128 * xx + 96:128 * xx + 128, 256:384] = groups[2][0:32]
            wr[64 + 16 * xx:80 + 16 * xx, 0:256] = txm[s, xx, 128:144, :]
            wr[64 + 16 * xx:80 + 16 * xx, 256:384] = groups[2][32:48]
        main = nt(sel_m[...], wm[...]).astype(BF)
        rest = jnp.zeros((128, 128), F32)
        for xx in range(4):
            um[s, :, 32 * xx:32 * xx + 32, :] = main[:, 128 * xx:128 * xx + 128].reshape(8, 32, 128)
            rest += nt(sel_x[xx], wm[128 * xx:128 * xx + 128, :])
        um[s, :, 128:144, :] = rest.astype(BF).reshape(8, 16, 128)
        low, high = wr[64:192, :], wr[0:128, :]
        rest = nt(sel_a[0], low) + nt(sel_a[1], high)
        um[s, :, 144:160, :] = rest.astype(BF).reshape(8, 16, 128)
        every = sel_x[0] + sel_x[1] + sel_x[2] + sel_x[3]
        rest = nt(every, low)
        keep = ((iota((128, 128), 1) >> 4) & 3) == ((iota((128, 128), 0) >> 2) & 3)
        um[s, :, 160:176, :] = jnp.where(keep, rest, 0.0).astype(BF).reshape(8, 16, 128)
        start(last_copies(s))
        tm[s, jme] = um[s, jme]

    def done(s):
        arrive(last_copies(s))
        def across(a, b):
            return jnp.concatenate([tm[s, j, a:b, :] for j in range(8)], axis=1)

        first = across(0, 144)
        packed = across(144, 160)
        second = jnp.concatenate([packed * mk[i:i + 1, :] for i in range(8)] + [across(160, 176)], axis=0)
        for n in range(3):
            cols = slice(384 * n, 384 * n + 384)
            tt[:, cols] = nn(first, s1[:, cols]) + nn(second, s2[:, cols])
        arrive(here_copies(s))
        dev = row * 8 + col
        row_limit = l_ref[s, dev // 16] - (dev % 16) * 36
        row_live = (iota((36, 1), 0) < row_limit).astype(F32)
        row_energy = er[s, 0:36, 0:1]
        lane = iota((1, 1152), 1)
        mains = [hm[s, yy].astype(F32) for yy in range(4)]
        rests = [hr[s, yy].astype(F32) for yy in range(4)]
        for xx in range(4):
            top, low = [], []
            for yy in range(4):
                top += [mains[yy][:, 256 * xx:256 * xx + 256], mains[yy][:, 1024 + 32 * xx:1056 + 32 * xx]]
                four = rests[yy][4 * xx:4 * xx + 4]
                low += [four[:, 0:256], four[:, 256 + 32 * xx:288 + 32 * xx]]
            top = jnp.concatenate(top, axis=1) + tt[32 * xx:32 * xx + 32, :]
            low = jnp.concatenate(low, axis=1) + tt[128 + 4 * xx:132 + 4 * xx, :]
            bound = jnp.where(lane < 576, l_ref[s, 2 * xx], l_ref[s, 2 * xx + 1] + 576)
            col_live = (lane < bound).astype(F32)
            energy = e_ref[pl.ds(s, 1), 1152 * xx:1152 * xx + 1152]
            cols = slice(1152 * xx, 1152 * xx + 1152)
            ob[s, 0:32, cols] = row_live[:32] * col_live * top / (row_energy[:32] + energy)
            ob[s, 32:36, cols] = row_live[32:] * col_live * low / (row_energy[32:] + energy)
        result_copy(s).start()

    def early_constants():
        i = iota((288, 288), 0)
        k = iota((288, 288), 1)
        head = 36 * natural(i >> 5) + (i & 31)
        tail = 36 * natural((i - 256) >> 2) + 32 + (i & 3)
        pm[...] = ones_where(k == jnp.where(i < 256, head, tail))

    def late_constants():
        i = iota((128, 128), 0)
        k = iota((128, 128), 1)
        qp[...] = ones_where(k == 32 * ((i >> 2) & 3) + 4 * (i >> 4) + (i & 3))
        i = iota((64, 64), 0)
        k = iota((64, 64), 1)
        fold[...] = ones_where(k == 16 * ((i >> 2) & 3) + 4 * (i >> 4) + (i & 3))
        i = iota((128, 512), 0)
        k = iota((128, 512), 1)
        lane = k & 127
        half = k >> 8
        hit = ((i >> 6) == half) & ((lane & 63) == (i & 63)) & ((lane >> 6) == ((k >> 7) & 1))
        ue[...] = ones_where(hit)

        def select(q, k):
            return (k == q) | ((k >= 256) & (k < 352) & (((k - 256) & 31) == q - 256))

        def shape3(n):
            return tuple(iota((8, n, 384), d) for d in range(3))

        j, t, k = shape3(32)
        sel_m[...] = ones_where(select(36 * natural(j) + t, k)).reshape(256, 384)
        j, t, k = shape3(16)
        for xx in range(4):
            hit = select(36 * natural(j) + 32 + (t & 3), k) & ((t >> 2) == xx)
            sel_x[xx] = ones_where(hit).reshape(128, 384)
        for h in range(2):
            sel_a[h] = ones_where(select(36 * natural(j) + 16 * h + t, k)).reshape(128, 384)
        wr[...] = jnp.zeros(wr.shape, BF)

        def fill(j, _):
            rows = rows_of(j, 128)
            r = iota((128, 1152), 0)
            k = iota((128, 1152), 1)
            base = 36 * natural(j)
            s1[rows, :] = ones_where(k == 288 * (r >> 5) + base + (r & 31))
            s2[rows, :] = ones_where(k == 288 * ((r >> 2) & 3) + base + 32 + (r & 3))
            return 0

        lax.fori_loop(0, 8, fill, 0)
        r = iota((16, 1024), 0)
        k = iota((16, 1024), 1)
        lane = k & 127
        quarter = ((lane >> 4) & 3) * 2 + (lane >> 6)
        mk[...] = ones_where(((r < 8) & (quarter == r)) | ((r >= 8) & ((lane >> 5) == r - 8)))
        dev = row * 8 + col
        pick = iota((40, 4608), 1) == iota((40, 4608), 0) + dev * 36
        for s in range(4):
            got = jnp.sum(jnp.where(pick, e_ref[s:s + 1, :], 0.0), axis=1, keepdims=True)
            er[s] = jnp.broadcast_to(got, (40, 128))

    early_constants()
    ready(0)
    barrier = pltpu.get_barrier_semaphore()
    partners = [at(d, 0, 0, 0) for d in (1, 2, 3)] + [at(0, d, 0, 0) for d in (1, 2, 3)]
    partners += [at(0, 0, i // 2, i % 2) for i in range(1, 8)]
    for p in partners:
        pl.semaphore_signal(barrier, 1, device_id=p, device_id_type=MESH)
    pl.semaphore_wait(barrier, len(partners))
    start(gather_own(0, 0))
    start(gather_own(0, 1))
    ready(1)
    late_constants()

    work = {
        "ready": ready, "relay": relay, "turn": turn, "done": done,
        "mul0": functools.partial(multiply, 0), "mul1": functools.partial(multiply, 1),
        "far0": functools.partial(far, 0), "far1": functools.partial(far, 1),
        "near0": functools.partial(near, 0), "near1": functools.partial(near, 1),
        "sum0": functools.partial(total, 0), "sum1": functools.partial(total, 1),
    }
    steps = ORDER[1:]

    def one_step(i, _):
        for name, what in work.items():
            places = [(at_step, s) for at_step, (n, s) in enumerate(steps) if n == name]
            now = functools.reduce(jnp.logical_or, [i == at_step for at_step, _ in places])
            s = sum(jnp.where(i == at_step, s, 0) for at_step, s in places)
            pl.when(now)(functools.partial(what, s))
        return 0

    lax.fori_loop(0, len(steps), one_step, 0)

    def drain(s, _):
        copies = gather_own(s, 0) + gather_own(s, 1) + gather_relay(s) + here_copies(s) + last_copies(s)
        for p in range(2):
            copies += swap(s, p) + zstep1(s, p) + zstep2(s, p)
        for p in range(3):
            copies += turn_copies(s, p)
        for cp in copies:
            cp.wait_send()
        result_copy(s).wait()
        return 0

    lax.fori_loop(0, 4, drain, 0)


def body(amplitudes, integrals, pair_energy, block_len):
    bf = lambda *shape: pltpu.VMEM(shape, BF)
    f32 = lambda *shape: pltpu.VMEM(shape, F32)
    dma = lambda *shape: pltpu.SemaphoreType.DMA(shape)
    scratch = [
        bf(4, 288, 576), bf(4, 288, 576),
        bf(4, 4, 1296, 128), bf(4, 4, 1296, 128),
        bf(1152, 768), bf(128, 512), bf(64, 128), bf(320, 768),
        bf(4, 4, 144, 1152), bf(4, 4, 144, 1152), f32(4, 144, 1152),
        bf(4, 144, 1152), bf(4, 2, 144, 1152), bf(4, 144, 1152), bf(4, 2, 144, 1152),
        f32(4, 144, 1152), bf(4, 144, 1152), bf(4, 4, 144, 256),
        bf(4, 4, 32, 1152), bf(4, 4, 16, 384), bf(4, 4, 16, 384),
        bf(4, 4, 144, 256), bf(4, 4, 48, 128), bf(4, 4, 48, 128),
        bf(512, 384), bf(192, 384), bf(4, 8, 176, 128), bf(4, 8, 176, 128), f32(144, 1152),
        bf(288, 288), bf(128, 128), bf(128, 512), bf(64, 64),
        bf(256, 384), bf(4, 128, 384), bf(2, 128, 384),
        bf(1024, 1152), bf(1024, 1152), bf(16, 1024), f32(4, 40, 128), f32(4, 36, 4608),
        dma(4, 2), dma(4, 2, 2, 2), dma(4, 2, 2, 2), dma(4, 2, 2), dma(4, 2, 2), dma(4, 2), dma(4, 2),
        dma(4, 2, 2), dma(4, 2, 2), dma(4, 2, 2), dma(4, 2, 2),
        dma(4, 3, 2), dma(4, 3, 2), dma(4, 3, 3), dma(4, 3, 3), dma(4, 7), dma(4, 7), dma(4),
    ]
    count, npairs = pair_energy.shape
    turned = pl.pallas_call(
        kernel,
        out_shape=jax.ShapeDtypeStruct((npairs // 128, count, npairs), F32),
        in_specs=[
            pl.BlockSpec(memory_space=pl.ANY),
            pl.BlockSpec(memory_space=pl.ANY),
            pl.BlockSpec(memory_space=pltpu.VMEM),
            pl.BlockSpec(memory_space=pltpu.SMEM),
        ],
        out_specs=pl.BlockSpec(memory_space=pl.ANY),
        scratch_shapes=scratch,
        compiler_params=pltpu.CompilerParams(
            collective_id=0, has_side_effects=True, vmem_limit_bytes=63 << 20
        ),
        name="cycle",
    )(amplitudes, jnp.swapaxes(integrals, 1, 2), pair_energy, block_len)
    return jnp.swapaxes(turned, 0, 1)


def solution(mesh):
    return jax.shard_map(
        body,
        mesh=mesh,
        in_specs=(P(None, "row", "col"), P(None, "col", "row"), P(), P()),
        out_specs=P(None, ("row", "col"), None),
        check_vma=False,
    )
```

```python
import functools

import jax
import jax.numpy as jnp
from jax import lax
from jax.experimental import pallas as pl
from jax.experimental.pallas import tpu as pltpu
from jax.sharding import PartitionSpec as P

MESH = pl.DeviceIdType.MESH
BF = jnp.bfloat16
F32 = jnp.float32
I32 = jnp.int32

PARTS = ((0, 80, 48), (80, 64, 32))
PIECES = ((0, 656), (656, 640))

TURNED = ((0, 160), (160, 176))

ORDER = (
    ("ready", 1), ("relay", 0), ("ready", 2), ("mul0", 0), ("mul1", 0), ("relay", 1), ("far0", 0), ("ready", 3),
    ("far1", 0), ("near0", 0), ("mul0", 1), ("far0", 1), ("relay", 2), ("near1", 0), ("mul1", 1), ("far1", 1),
    ("near0", 1), ("mul0", 2), ("relay", 3), ("far0", 2), ("near1", 1), ("sum0", 0), ("mul1", 2), ("far1", 2),
    ("near0", 2), ("mul0", 3), ("near1", 2), ("mul1", 3), ("sum1", 0), ("sum0", 1), ("far0", 3), ("sum0", 2),
    ("far1", 3), ("turn", 0), ("near0", 3), ("here", 0), ("sum1", 1), ("near1", 3), ("drain", 0), ("sum1", 2),
    ("done", 0), ("turn", 1), ("turn", 2), ("sum0", 3), ("here", 1), ("sum1", 3), ("here", 2), ("turn", 3),
    ("drain", 1), ("done", 1), ("drain", 2), ("here", 3), ("drain", 3), ("done", 2), ("done", 3),
)


def nt(a, b):
    return lax.dot_general(a, b, (((1,), (1,)), ((), ())), preferred_element_type=F32)


def nn(a, b):
    return jnp.dot(a, b, preferred_element_type=F32)


def iota(shape, dim):
    return lax.broadcasted_iota(I32, shape, dim)


def natural(j):
    return 2 * (j & 3) + (j >> 2)


def ones_where(hit):
    return hit.astype(F32).astype(BF)


def kernel(
    a_hbm, b_hbm, e_ref, l_ref, o_hbm,
    av, bv, ra, rb, rhs, grem, gremf, lhs, ps, cx, pf, q1, q2, z1, z2, own, db, dx, hx, hm, txm,
    wm, wr, um, tm, sc, pm, qp, ue, fold, sel_m, sel_x, sel_a, s1, s2, mk, er, ob,
    lsem, gos, gor, grs, grr, cs, cr, z1s, z1r, z2s, z2r, hs, hrr, xs, xr, ts, tsr, osem,
):
    row = lax.axis_index("row")
    col = lax.axis_index("col")
    x, y = row >> 2, row & 3
    z, c = col >> 1, col & 1
    jme = c * 4 + z

    def at(dx, dy, dz, dc):
        return (((x + dx) & 3) * 4 + ((y + dy) & 3), ((z + dz) & 3) * 2 + ((c + dc) & 1))

    def remote(src, dst, ssem, rsem, where):
        return pltpu.make_async_remote_copy(
            src_ref=src, dst_ref=dst, send_sem=ssem, recv_sem=rsem, device_id=where, device_id_type=MESH
        )

    def load(s):
        return (
            pltpu.make_async_copy(a_hbm.at[s], av.at[s], lsem.at[s, 0]),
            pltpu.make_async_copy(b_hbm.at[s], bv.at[s], lsem.at[s, 1]),
        )

    for s in range(4):
        for cp in load(s):
            cp.start()

    def rows_of(v, size):
        return pl.ds(pl.multiple_of(v * size, size), size)

    def gather_own(s, which):
        out = []
        for d, step in ((0, 1), (1, 3)):
            first, size = PIECES[d ^ which]
            rows = pl.ds(first, size)
            blk = ra.at[s, y, rows, :]
            out.append(remote(blk, blk, gos.at[s, d, which, 0], gor.at[s, d, which, 0], at(0, step, 0, 0)))
            blk = rb.at[s, x, rows, :]
            out.append(remote(blk, blk, gos.at[s, d, which, 1], gor.at[s, d, which, 1], at(step, 0, 0, 0)))
        return out

    def gather_relay(s):
        out = []
        for d, step in ((0, 1), (1, 3)):
            first, size = PIECES[d]
            rows = pl.ds(first, size)
            blk = ra.at[s, (y + 4 - step) & 3, rows, :]
            out.append(remote(blk, blk, grs.at[s, d, 0], grr.at[s, d, 0], at(0, step, 0, 0)))
            blk = rb.at[s, (x + 4 - step) & 3, rows, :]
            out.append(remote(blk, blk, grs.at[s, d, 1], grr.at[s, d, 1], at(step, 0, 0, 0)))
        return out

    def swap(s, p):
        rows = pl.ds(*PARTS[p][:2])
        out = []
        for i, step in enumerate((2, 1, 3, 0)):
            zz = (z + step) & 3
            out.append(remote(
                ps.at[s, zz, rows, :], cx.at[s, zz, rows, :], cs.at[s, p, i], cr.at[s, p, i], at(0, 0, 0, 1)
            ))
        return out

    def steps_of(s):
        odd = s & 1
        return 1 + 2 * odd, 3 - 2 * odd

    def zstep1(s, p):
        first, size, up = PARTS[p]
        out = []
        for d, step, rows in zip((0, 1), steps_of(s), (pl.ds(first, up), pl.ds(first + up, size - up))):
            out.append(remote(
                q1.at[s, rows, :], z1.at[s, rows, :], z1s.at[s, p, d], z1r.at[s, p, d], at(0, 0, step, 0)
            ))
        return out

    def zstep2(s, p):
        rows = pl.ds(*PARTS[p][:2])
        return [
            remote(q2.at[s, d, rows, :], z2.at[s, d, rows, :], z2s.at[s, p, d], z2r.at[s, p, d], at(0, 0, step, 0))
            for d, step in zip((0, 1), steps_of(s))
        ]

    def here_copies(s):
        return [
            remote(hx.at[s, (y + d) & 3], hm.at[s, y], hs.at[s, d - 1], hrr.at[s, d - 1], at(0, d, 0, 0))
            for d in (1, 2, 3)
        ]

    def turn_copies(s, p):
        rows = pl.ds(*TURNED[p])
        return [
            remote(
                dx.at[s, (x + d) & 3, rows, :], txm.at[s, x, rows, :],
                xs.at[s, d - 1, p], xr.at[s, d - 1, p], at(d, 0, 0, 0),
            )
            for d in (1, 2, 3)
        ]

    def last_copies(s):
        out = []
        for i in (2, 6, 4, 3, 7, 5, 1):
            dz, dc = i // 2, i % 2
            jto = ((c + dc) & 1) * 4 + ((z + dz) & 3)
            out.append(remote(
                um.at[s, jto], tm.at[s, jme], ts.at[s, i - 1], tsr.at[s, i - 1], at(0, 0, dz, dc)
            ))
        return out

    def result_copy(s):
        return pltpu.make_async_copy(ob.at[s], o_hbm.at[:, s, :], osem.at[s])

    def start(copies):
        for cp in copies:
            cp.start()

    def arrive(copies):
        for cp in copies:
            cp.wait_recv()

    def fold_lanes(low, high):
        return jnp.concatenate([low, high], axis=1)

    def ready(s):
        for cp in load(s):
            cp.wait()
        limit = l_ref[s, col]
        masked = jnp.where(iota((288, 576), 1) < limit, av[s].astype(F32), 0.0).astype(BF)
        turned = nn(pm[...], masked)
        b = bv[s]
        for k in range(4):
            ra[s, y, 288 * k:288 * k + 288, :] = turned[:, 128 * k:128 * k + 128].astype(BF)
            rb[s, x, 288 * k:288 * k + 288, :] = b[:, 128 * k:128 * k + 128]
        rest = turned[:, 512:576]
        ra[s, y, 1152:1280, :] = fold_lanes(rest[0:128], rest[128:256]).astype(BF)
        ra[s, y, 1280:1296, :] = fold_lanes(rest[256:272], rest[272:288]).astype(BF)
        rest = b[:, 512:576].astype(F32)
        rb[s, x, 1152:1296, :] = fold_lanes(rest[0:144], rest[144:288]).astype(BF)

    def relay(s):
        arrive(gather_own(s, 0))
        start(gather_relay(s))

        @pl.when(s < 3)
        def _():
            start(gather_own(s + 1, 0))
            start(gather_own(s + 1, 1))

    def unfold(s):
        got = nn(rb[s, :, 1152:1296, :].reshape(576, 128), ue[...]).astype(BF)
        for xx in range(4):
            for k in range(4):
                lanes = slice(128 * k, 128 * k + 128)
                rhs[256 * xx:256 * xx + 256, lanes] = rb[s, xx, 288 * k:288 * k + 256, :]
                rhs[1024 + 32 * xx:1056 + 32 * xx, lanes] = rb[s, xx, 288 * k + 256:288 * k + 288, :]
            low, high = got[144 * xx:144 * xx + 144, 0:256], got[144 * xx:144 * xx + 144, 256:512]
            rhs[256 * xx:256 * xx + 144, 512:768] = low
            rhs[256 * xx + 144:256 * xx + 256, 512:768] = high[0:112]
            rhs[1024 + 32 * xx:1056 + 32 * xx, 512:768] = high[112:144]
        for k in range(4):
            grem[:, 128 * k:128 * k + 128] = nn(
                qp[...], ra[s, :, 288 * k + 256:288 * k + 288, :].reshape(128, 128)
            ).astype(BF)
        gremf[...] = nn(fold[...], ra[s, :, 1280:1296, :].reshape(64, 128)).astype(BF)

    def gather_lhs(s, p, h):
        first, size, _ = PARTS[p]
        lanes = pl.ds(pl.multiple_of(512 + 128 * h, 128), 128)
        lhs[:, pl.ds(pl.multiple_of(640 - 128 * h, 128), 128)] = jnp.zeros((320, 128), BF)
        for zz in range(4):
            at_row = size * zz
            j = h * 4 + zz
            spans = ((0, 0, 32), (1, 0, 32), (2, 0, 16)) if p == 0 else ((2, 16, 16), (3, 0, 32))
            for yy, skip, n in spans:
                for k in range(4):
                    rows = pl.ds(pl.multiple_of(288 * k + 32 * j + skip, 16), n)
                    lhs[at_row:at_row + n, 128 * k:128 * k + 128] = ra[s, yy, rows, :]
                lhs[at_row:at_row + n, lanes] = ra[s, yy, 1152 + 32 * zz + skip:1152 + 32 * zz + skip + n, :]
                at_row += n
            if p == 1:
                lhs[at_row:at_row + 16, 0:512] = grem[rows_of(j, 16), :]
                lhs[at_row:at_row + 16, lanes] = gremf[16 * zz:16 * zz + 16, :]

    def multiply(p, s):
        if p == 0:
            arrive(gather_own(s, 1))
            arrive(gather_relay(s))
            unfold(s)
        first, size, _ = PARTS[p]
        rows = slice(first, first + size)

        def product(h):
            gather_lhs(s, p, h)
            return nt(lhs[0:4 * size, :], rhs[...]).reshape(4, size, 1152)

        ps[s, :, rows, :] = product(1 - c).astype(BF)
        start(swap(s, p))
        pf[:, rows, :] = product(c)

    def each16(first, count, what):
        def one(i, _):
            what(pl.ds(pl.multiple_of(first + i * 16, 16), 16))
            return 0

        lax.fori_loop(0, count // 16, one, 0)

    def here_sum(s, zz, rows):
        return pf[zz, rows, :] + cx[s, zz, rows, :].astype(F32)

    def far(p, s):
        first, size, _ = PARTS[p]
        arrive(swap(s, p)[:1])

        def add(rows):
            q1[s, rows, :] = here_sum(s, (z + 2) & 3, rows).astype(BF)

        each16(first, size, add)
        start(zstep1(s, p))

    def near(p, s):
        first, size, up = PARTS[p]
        arrive(swap(s, p)[1:])
        arrive(zstep1(s, p))
        zup, zdown = ((z + step) & 3 for step in steps_of(s))

        def add_up(rows):
            q2[s, 0, rows, :] = (here_sum(s, zup, rows) + z1[s, rows, :].astype(F32)).astype(BF)
            q2[s, 1, rows, :] = here_sum(s, zdown, rows).astype(BF)

        def add_down(rows):
            q2[s, 0, rows, :] = here_sum(s, zup, rows).astype(BF)
            q2[s, 1, rows, :] = (here_sum(s, zdown, rows) + z1[s, rows, :].astype(F32)).astype(BF)

        each16(first, up, add_up)
        each16(first + up, size - up, add_down)
        start(zstep2(s, p))

        def keep(rows):
            own[s, rows, :] = here_sum(s, z, rows)

        each16(first, size, keep)

    def total(p, s):
        first, size, _ = PARTS[p]
        base = TURNED[p][0]
        arrive(zstep2(s, p))

        def add(i, _):
            rows = pl.ds(pl.multiple_of(first + 16 * i, 16), 16)
            v = own[s, rows, :] + z2[s, 0, rows, :].astype(F32) + z2[s, 1, rows, :].astype(F32)
            v = v.astype(BF)
            db[s, rows, :] = v
            for xx in range(4):
                for k in range(2):
                    to = pl.ds(pl.multiple_of(base + size * k + 16 * i, 16), 16)
                    dx[s, xx, to, :] = v[:, 256 * xx + 128 * k:256 * xx + 128 * k + 128]
            return 0

        lax.fori_loop(0, size // 16, add, 0)
        if p == 1:
            tail = db[s, :, 1024:1152].astype(F32)
            for xx in range(4):
                lanes = slice(32 * xx, 32 * xx + 32)
                packed = [tail[48 * g:48 * g + 48, lanes] for g in range(3)]
                packed.append(jnp.zeros((48, 32), F32))
                dx[s, xx, 288:336, :] = jnp.concatenate(packed, axis=1).astype(BF)
        start(turn_copies(s, p))
        span = slice(base, base + TURNED[p][1])
        txm[s, x, span, :] = dx[s, x, span, :]
        if p == 1:
            for yy in range(4):
                for k in range(9):
                    hx[s, yy, 32 * k:32 * k + 32, :] = db[s, 32 * yy:32 * yy + 32, 128 * k:128 * k + 128]
                mine = db[s, 128:144, :].astype(F32)[4 * yy:4 * yy + 4]
                for k in range(3):
                    lanes = [128 * k + 256 * xx if k < 2 else 1024 for xx in range(4)]
                    hx[s, yy, 288 + 16 * k:304 + 16 * k, :] = jnp.concatenate(
                        [mine[:, i:i + 128] for i in lanes], axis=0
                    ).astype(BF)
            start(here_copies(s))
            hm[s, y] = hx[s, y]

    def turn(s):
        for p in range(2):
            arrive(turn_copies(s, p))
        for xx in range(4):
            packed = txm[s, xx, 288:336, :]
            groups = [packed * mk[8 + g:9 + g, 0:128] for g in range(3)]
            at_row = 128 * xx
            for k in range(2):
                lanes = slice(128 * k, 128 * k + 128)
                wm[at_row:at_row + 80, lanes] = txm[s, xx, 80 * k:80 * k + 80, :]
                wm[at_row + 80:at_row + 128, lanes] = txm[s, xx, 160 + 64 * k:208 + 64 * k, :]
                wr[64 + 16 * xx:80 + 16 * xx, lanes] = txm[s, xx, 208 + 64 * k:224 + 64 * k, :]
            wm[at_row:at_row + 48, 256:384] = groups[0]
            wm[at_row + 48:at_row + 96, 256:384] = groups[1]
            wm[at_row + 96:at_row + 128, 256:384] = groups[2][0:32]
            wr[64 + 16 * xx:80 + 16 * xx, 256:384] = groups[2][32:48]
        main = nt(sel_m[...], wm[...]).astype(BF)
        rest = jnp.zeros((128, 128), F32)
        for xx in range(4):
            um[s, :, 32 * xx:32 * xx + 32, :] = main[:, 128 * xx:128 * xx + 128].reshape(8, 32, 128)
            rest += nt(sel_x[xx], wm[128 * xx:128 * xx + 128, :])
        um[s, :, 128:144, :] = rest.astype(BF).reshape(8, 16, 128)
        low, high = wr[64:192, :], wr[0:128, :]
        rest = nt(sel_a[0], low) + nt(sel_a[1], high)
        um[s, :, 144:160, :] = rest.astype(BF).reshape(8, 16, 128)
        every = sel_x[0] + sel_x[1] + sel_x[2] + sel_x[3]
        rest = nt(every, low)
        keep = ((iota((128, 128), 1) >> 4) & 3) == ((iota((128, 128), 0) >> 2) & 3)
        um[s, :, 160:176, :] = jnp.where(keep, rest, 0.0).astype(BF).reshape(8, 16, 128)
        start(last_copies(s))
        tm[s, jme] = um[s, jme]

    def here(s):
        arrive(here_copies(s))
        slot = s & 1
        dev = row * 8 + col
        row_limit = l_ref[s, dev >> 4] - (dev & 15) * 36
        row_live = (iota((36, 1), 0) < row_limit).astype(F32)
        row_energy = er[s, 0:36, 0:1]
        lane = iota((1, 1152), 1)
        tiles = [[hm[s, yy, 32 * k:32 * k + 32, :].astype(F32) for k in range(9)] for yy in range(4)]
        rests = [[hm[s, yy, 288 + 16 * k:304 + 16 * k, :].astype(F32) for k in range(3)] for yy in range(4)]
        for xx in range(4):
            top, low = [], []
            for yy in range(4):
                last = slice(32 * xx, 32 * xx + 32)
                top += [tiles[yy][2 * xx], tiles[yy][2 * xx + 1], tiles[yy][8][:, last]]
                low += [v[4 * xx:4 * xx + 4] for v in rests[yy][:2]] + [rests[yy][2][4 * xx:4 * xx + 4, last]]
            cols = slice(1152 * xx, 1152 * xx + 1152)
            ob[s, 0:32, cols] = jnp.concatenate(top, axis=1)
            ob[s, 32:36, cols] = jnp.concatenate(low, axis=1)
            bound = jnp.where(lane < 576, l_ref[s, 2 * xx], l_ref[s, 2 * xx + 1] + 576)
            col_live = (lane < bound).astype(F32)
            sc[slot, :, cols] = row_live * col_live / (row_energy + e_ref[pl.ds(s, 1), cols])

    def done(s):
        slot = s & 1
        arrive(last_copies(s))

        def across(a, b):
            return jnp.concatenate([tm[s, j, a:b, :] for j in range(8)], axis=1)

        first = across(0, 144)
        packed = across(144, 160)
        second = jnp.concatenate([packed * mk[i:i + 1, :] for i in range(8)] + [across(160, 176)], axis=0)
        for n in range(3):
            cols = slice(384 * n, 384 * n + 384)
            got = nn(first, s1[:, cols]) + nn(second, s2[:, cols])
            for xx in range(4):
                cols = slice(1152 * xx + 384 * n, 1152 * xx + 384 * n + 384)
                ob[s, 0:32, cols] = (ob[s, 0:32, cols] + got[32 * xx:32 * xx + 32]) * sc[slot, 0:32, cols]
                ob[s, 32:36, cols] = (ob[s, 32:36, cols] + got[128 + 4 * xx:132 + 4 * xx]) * sc[slot, 32:36, cols]
        result_copy(s).start()

    def early_constants():
        i = iota((288, 288), 0)
        k = iota((288, 288), 1)
        head = 36 * natural(i >> 5) + (i & 31)
        tail = 36 * natural((i - 256) >> 2) + 32 + (i & 3)
        pm[...] = ones_where(k == jnp.where(i < 256, head, tail))

    def late_constants():
        i = iota((128, 128), 0)
        k = iota((128, 128), 1)
        qp[...] = ones_where(k == 32 * ((i >> 2) & 3) + 4 * (i >> 4) + (i & 3))
        i = iota((64, 64), 0)
        k = iota((64, 64), 1)
        fold[...] = ones_where(k == 16 * ((i >> 2) & 3) + 4 * (i >> 4) + (i & 3))
        i = iota((128, 512), 0)
        k = iota((128, 512), 1)
        lane = k & 127
        half = k >> 8
        hit = ((i >> 6) == half) & ((lane & 63) == (i & 63)) & ((lane >> 6) == ((k >> 7) & 1))
        ue[...] = ones_where(hit)

        def select(q, k):
            return (k == q) | ((k >= 256) & (k < 352) & (((k - 256) & 31) == q - 256))

        def shape3(n):
            return tuple(iota((8, n, 384), d) for d in range(3))

        j, t, k = shape3(32)
        sel_m[...] = ones_where(select(36 * natural(j) + t, k)).reshape(256, 384)
        j, t, k = shape3(16)
        for xx in range(4):
            hit = select(36 * natural(j) + 32 + (t & 3), k) & ((t >> 2) == xx)
            sel_x[xx] = ones_where(hit).reshape(128, 384)
        for h in range(2):
            sel_a[h] = ones_where(select(36 * natural(j) + 16 * h + t, k)).reshape(128, 384)
        wr[...] = jnp.zeros(wr.shape, BF)

        def fill(j, _):
            rows = rows_of(j, 128)
            r = iota((128, 1152), 0)
            k = iota((128, 1152), 1)
            base = 36 * natural(j)
            s1[rows, :] = ones_where(k == 288 * (r >> 5) + base + (r & 31))
            s2[rows, :] = ones_where(k == 288 * ((r >> 2) & 3) + base + 32 + (r & 3))
            return 0

        lax.fori_loop(0, 8, fill, 0)
        r = iota((16, 1024), 0)
        k = iota((16, 1024), 1)
        lane = k & 127
        quarter = ((lane >> 4) & 3) * 2 + (lane >> 6)
        mk[...] = ones_where(((r < 8) & (quarter == r)) | ((r >= 8) & ((lane >> 5) == r - 8)))
        dev = row * 8 + col
        pick = iota((40, 4608), 1) == iota((40, 4608), 0) + dev * 36
        for s in range(4):
            got = jnp.sum(jnp.where(pick, e_ref[s:s + 1, :], 0.0), axis=1, keepdims=True)
            er[s] = jnp.broadcast_to(got, (40, 128))

    early_constants()
    ready(0)
    barrier = pltpu.get_barrier_semaphore()
    partners = [at(d, 0, 0, 0) for d in (1, 2, 3)] + [at(0, d, 0, 0) for d in (1, 2, 3)]
    partners += [at(0, 0, i // 2, i % 2) for i in range(1, 8)]
    for p in partners:
        pl.semaphore_signal(barrier, 1, device_id=p, device_id_type=MESH)
    pl.semaphore_wait(barrier, len(partners))
    start(gather_own(0, 0))
    start(gather_own(0, 1))
    ready(1)
    late_constants()

    def drain(s):
        copies = gather_own(s, 0) + gather_own(s, 1) + gather_relay(s) + here_copies(s)
        for p in range(2):
            copies += swap(s, p) + zstep1(s, p) + zstep2(s, p) + turn_copies(s, p)
        for cp in copies:
            cp.wait_send()

        @pl.when(s < 3)
        def _():
            for cp in last_copies(s):
                cp.wait_send()

    work = {
        "ready": ready, "relay": relay, "turn": turn, "here": here, "done": done, "drain": drain,
        "mul0": functools.partial(multiply, 0), "mul1": functools.partial(multiply, 1),
        "far0": functools.partial(far, 0), "far1": functools.partial(far, 1),
        "near0": functools.partial(near, 0), "near1": functools.partial(near, 1),
        "sum0": functools.partial(total, 0), "sum1": functools.partial(total, 1),
    }
    steps = ORDER[1:]

    def one_step(i, _):
        for name, what in work.items():
            places = [(at_step, s) for at_step, (n, s) in enumerate(steps) if n == name]
            now = functools.reduce(jnp.logical_or, [i == at_step for at_step, _ in places])
            s = sum(jnp.where(i == at_step, s, 0) for at_step, s in places)
            pl.when(now)(functools.partial(what, s))
        return 0

    lax.fori_loop(0, len(steps), one_step, 0)

    for cp in last_copies(3):
        cp.wait_send()
    for s in range(4):
        result_copy(s).wait()


def body(amplitudes, integrals, pair_energy, block_len):
    bf = lambda *shape: pltpu.VMEM(shape, BF)
    f32 = lambda *shape: pltpu.VMEM(shape, F32)
    dma = lambda *shape: pltpu.SemaphoreType.DMA(shape)
    scratch = [
        bf(4, 288, 576), bf(4, 288, 576),
        bf(4, 4, 1296, 128), bf(4, 4, 1296, 128),
        bf(1152, 768), bf(128, 512), bf(64, 128), bf(320, 768),
        bf(4, 4, 144, 1152), bf(4, 4, 144, 1152), f32(4, 144, 1152),
        bf(4, 144, 1152), bf(4, 2, 144, 1152), bf(4, 144, 1152), bf(4, 2, 144, 1152),
        f32(4, 144, 1152), bf(4, 144, 1152), bf(4, 4, 336, 128),
        bf(4, 4, 336, 128), bf(4, 4, 336, 128), bf(4, 4, 336, 128),
        bf(512, 384), bf(192, 384), bf(4, 8, 176, 128), bf(4, 8, 176, 128), f32(2, 36, 4608),
        bf(288, 288), bf(128, 128), bf(128, 512), bf(64, 64),
        bf(256, 384), bf(4, 128, 384), bf(2, 128, 384),
        bf(1024, 1152), bf(1024, 1152), bf(16, 1024), f32(4, 40, 128), f32(4, 36, 4608),
        dma(4, 2), dma(4, 2, 2, 2), dma(4, 2, 2, 2), dma(4, 2, 2), dma(4, 2, 2), dma(4, 2, 4), dma(4, 2, 4),
        dma(4, 2, 2), dma(4, 2, 2), dma(4, 2, 2), dma(4, 2, 2),
        dma(4, 3), dma(4, 3), dma(4, 3, 2), dma(4, 3, 2), dma(4, 7), dma(4, 7), dma(4),
    ]
    count, npairs = pair_energy.shape
    turned = pl.pallas_call(
        kernel,
        out_shape=pltpu.VMEM((npairs // 128, count, npairs), F32),
        in_specs=[
            pl.BlockSpec(memory_space=pl.ANY),
            pl.BlockSpec(memory_space=pl.ANY),
            pl.BlockSpec(memory_space=pltpu.VMEM),
            pl.BlockSpec(memory_space=pltpu.SMEM),
        ],
        out_specs=pl.BlockSpec(memory_space=pltpu.VMEM),
        scratch_shapes=scratch,
        compiler_params=pltpu.CompilerParams(
            collective_id=0, has_side_effects=True, vmem_limit_bytes=60 << 20
        ),
        name="cycle",
    )(amplitudes, jnp.swapaxes(integrals, 1, 2), pair_energy, block_len)
    return jnp.swapaxes(turned, 0, 1)


def solution(mesh):
    return jax.shard_map(
        body,
        mesh=mesh,
        in_specs=(P(None, "row", "col"), P(None, "col", "row"), P(), P()),
        out_specs=P(None, ("row", "col"), None),
        check_vma=False,
    )
```

```python
import functools

import jax
import jax.numpy as jnp
from jax import lax
from jax.experimental import pallas as pl
from jax.experimental.pallas import tpu as pltpu
from jax.sharding import PartitionSpec as P

MESH = pl.DeviceIdType.MESH
BF = jnp.bfloat16
F32 = jnp.float32
I32 = jnp.int32

PARTS = ((0, 80, 48), (80, 64, 32))
PIECES = ((0, 656), (656, 640))

TURNED = ((0, 160), (160, 176))

ORDER = (
    ("ready", 1), ("relay", 0), ("ready", 2), ("mul0", 0), ("mul1", 0), ("relay", 1), ("far0", 0), ("ready", 3),
    ("far1", 0), ("near0", 0), ("mul0", 1), ("far0", 1), ("relay", 2), ("near1", 0), ("mul1", 1), ("far1", 1),
    ("near0", 1), ("mul0", 2), ("relay", 3), ("far0", 2), ("near1", 1), ("sum0", 0), ("mul1", 2), ("far1", 2),
    ("near0", 2), ("mul0", 3), ("near1", 2), ("mul1", 3), ("sum1", 0), ("sum0", 1), ("far0", 3), ("sum0", 2),
    ("far1", 3), ("turn", 0), ("near0", 3), ("here", 0), ("sum1", 1), ("near1", 3), ("drain", 0), ("sum1", 2),
    ("done", 0), ("turn", 1), ("turn", 2), ("sum0", 3), ("here", 1), ("sum1", 3), ("here", 2), ("turn", 3),
    ("drain", 1), ("done", 1), ("drain", 2), ("here", 3), ("drain", 3), ("done", 2), ("done", 3),
)


def nt(a, b):
    return lax.dot_general(a, b, (((1,), (1,)), ((), ())), preferred_element_type=F32)


def nn(a, b):
    return jnp.dot(a, b, preferred_element_type=F32)


def iota(shape, dim):
    return lax.broadcasted_iota(I32, shape, dim)


def natural(j):
    return 2 * (j & 3) + (j >> 2)


def ones_where(hit):
    return hit.astype(F32).astype(BF)


def kernel(
    a_hbm, b_hbm, e_ref, l_ref, o_ref,
    av, bv, ra, rb, rhs, grem, gremf, lhs, ps, cx, pf, q1, q2, z1, z2, own, db, dx, hx, hm, txm,
    wm, wr, um, tm, sc, pm, qp, ue, fold, sel_m, sel_x, sel_a, s12, mk, er, ob,
    lsem, gos, gor, grs, grr, cs, cr, z1s, z1r, z2s, z2r, hs, hrr, xs, xr, ts, tsr, osem,
):
    row = lax.axis_index("row")
    col = lax.axis_index("col")
    x, y = row >> 2, row & 3
    z, c = col >> 1, col & 1
    jme = c * 4 + z

    def at(dx, dy, dz, dc):
        return (((x + dx) & 3) * 4 + ((y + dy) & 3), ((z + dz) & 3) * 2 + ((c + dc) & 1))

    def remote(src, dst, ssem, rsem, where):
        return pltpu.make_async_remote_copy(
            src_ref=src, dst_ref=dst, send_sem=ssem, recv_sem=rsem, device_id=where, device_id_type=MESH
        )

    def load(s):
        return (
            pltpu.make_async_copy(a_hbm.at[s], av.at[s], lsem.at[s, 0]),
            pltpu.make_async_copy(b_hbm.at[s], bv.at[s], lsem.at[s, 1]),
        )

    for cp in load(0):
        cp.start()

    barrier = pltpu.get_barrier_semaphore()
    partners = [at(d, 0, 0, 0) for d in (1, 2, 3)] + [at(0, d, 0, 0) for d in (1, 2, 3)]
    partners += [at(0, 0, i // 2, i % 2) for i in range(1, 8)]
    for p in partners:
        pl.semaphore_signal(barrier, 1, device_id=p, device_id_type=MESH)

    def rows_of(v, size):
        return pl.ds(pl.multiple_of(v * size, size), size)

    def gather_own(s, which):
        out = []
        for d, step in ((0, 1), (1, 3)):
            first, size = PIECES[d ^ which]
            rows = pl.ds(first, size)
            blk = ra.at[s, y, rows, :]
            out.append(remote(blk, blk, gos.at[s, d, which, 0], gor.at[s, d, which, 0], at(0, step, 0, 0)))
            blk = rb.at[s, x, rows, :]
            out.append(remote(blk, blk, gos.at[s, d, which, 1], gor.at[s, d, which, 1], at(step, 0, 0, 0)))
        return out

    def gather_relay(s):
        out = []
        for d, step in ((0, 1), (1, 3)):
            first, size = PIECES[d]
            rows = pl.ds(first, size)
            blk = ra.at[s, (y + 4 - step) & 3, rows, :]
            out.append(remote(blk, blk, grs.at[s, d, 0], grr.at[s, d, 0], at(0, step, 0, 0)))
            blk = rb.at[s, (x + 4 - step) & 3, rows, :]
            out.append(remote(blk, blk, grs.at[s, d, 1], grr.at[s, d, 1], at(step, 0, 0, 0)))
        return out

    def swap(s, p):
        rows = pl.ds(*PARTS[p][:2])
        out = []
        for i, step in enumerate((2, 1, 3, 0)):
            zz = (z + step) & 3
            out.append(remote(
                ps.at[s, zz, rows, :], cx.at[s, zz, rows, :], cs.at[s, p, i], cr.at[s, p, i], at(0, 0, 0, 1)
            ))
        return out

    def steps_of(s):
        odd = s & 1
        return 1 + 2 * odd, 3 - 2 * odd

    def zstep1(s, p):
        first, size, up = PARTS[p]
        out = []
        for d, step, rows in zip((0, 1), steps_of(s), (pl.ds(first, up), pl.ds(first + up, size - up))):
            out.append(remote(
                q1.at[s, rows, :], z1.at[s, rows, :], z1s.at[s, p, d], z1r.at[s, p, d], at(0, 0, step, 0)
            ))
        return out

    def zstep2(s, p):
        rows = pl.ds(*PARTS[p][:2])
        return [
            remote(q2.at[s, d, rows, :], z2.at[s, d, rows, :], z2s.at[s, p, d], z2r.at[s, p, d], at(0, 0, step, 0))
            for d, step in zip((0, 1), steps_of(s))
        ]

    def here_copies(s):
        return [
            remote(hx.at[s, (y + d) & 3], hm.at[s, y], hs.at[s, d - 1], hrr.at[s, d - 1], at(0, d, 0, 0))
            for d in (1, 2, 3)
        ]

    def turn_copies(s, p):
        rows = pl.ds(*TURNED[p])
        return [
            remote(
                dx.at[s, (x + d) & 3, rows, :], txm.at[s, x, rows, :],
                xs.at[s, d - 1, p], xr.at[s, d - 1, p], at(d, 0, 0, 0),
            )
            for d in (1, 2, 3)
        ]

    def last_copies(s):
        out = []
        for i in (2, 6, 4, 3, 7, 5, 1):
            dz, dc = i // 2, i % 2
            jto = ((c + dc) & 1) * 4 + ((z + dz) & 3)
            out.append(remote(
                um.at[s, jto], tm.at[s, jme], ts.at[s, i - 1], tsr.at[s, i - 1], at(0, 0, dz, dc)
            ))
        return out

    def result_copy(s, xx):
        cols = pl.ds(1152 * xx, 1152)
        return pltpu.make_async_copy(ob.at[s, :, cols], o_ref.at[:, s, cols], osem.at[s, xx])

    def start(copies):
        for cp in copies:
            cp.start()

    def arrive(copies):
        for cp in copies:
            cp.wait_recv()

    def fold_lanes(low, high):
        return jnp.concatenate([low, high], axis=1)

    def ready(s):
        for cp in load(s):
            cp.wait()
        limit = l_ref[s, col]
        masked = jnp.where(iota((288, 576), 1) < limit, av[s].astype(F32), 0.0).astype(BF)
        turned = nn(pm[...], masked)
        b = bv[s]
        for k in range(4):
            ra[s, y, 288 * k:288 * k + 288, :] = turned[:, 128 * k:128 * k + 128].astype(BF)
            rb[s, x, 288 * k:288 * k + 288, :] = b[:, 128 * k:128 * k + 128]
        rest = turned[:, 512:576]
        ra[s, y, 1152:1280, :] = fold_lanes(rest[0:128], rest[128:256]).astype(BF)
        ra[s, y, 1280:1296, :] = fold_lanes(rest[256:272], rest[272:288]).astype(BF)
        rest = b[:, 512:576].astype(F32)
        rb[s, x, 1152:1296, :] = fold_lanes(rest[0:144], rest[144:288]).astype(BF)

    def relay(s):
        arrive(gather_own(s, 0))
        start(gather_relay(s))

        @pl.when(s < 3)
        def _():
            start(gather_own(s + 1, 0))
            start(gather_own(s + 1, 1))

    def unfold_block(s, xx):
        got = nn(rb[s, xx, 1152:1296, :], ue[...]).astype(BF)
        low, high = got[:, 0:256], got[:, 256:512]

        def main(first, size):
            return pl.ds(pl.multiple_of(256 * xx + first, 16), size)

        rest = pl.ds(pl.multiple_of(1024 + 32 * xx, 32), 32)
        for k in range(4):
            lanes = slice(128 * k, 128 * k + 128)
            rhs[main(0, 256), lanes] = rb[s, xx, 288 * k:288 * k + 256, :]
            rhs[rest, lanes] = rb[s, xx, 288 * k + 256:288 * k + 288, :]
        rhs[main(0, 144), 512:768] = low
        rhs[main(144, 112), 512:768] = high[0:112]
        rhs[rest, 512:768] = high[112:144]

    def unfold(s):
        unfold_block(s, (x + 2) & 3)
        for k in range(4):
            grem[:, 128 * k:128 * k + 128] = nn(
                qp[...], ra[s, :, 288 * k + 256:288 * k + 288, :].reshape(128, 128)
            ).astype(BF)
        gremf[...] = nn(fold[...], ra[s, :, 1280:1296, :].reshape(64, 128)).astype(BF)

    def gather_lhs(s, p, h):
        first, size, _ = PARTS[p]
        lanes = pl.ds(pl.multiple_of(512 + 128 * h, 128), 128)
        lhs[:, pl.ds(pl.multiple_of(640 - 128 * h, 128), 128)] = jnp.zeros((320, 128), BF)
        for zz in range(4):
            at_row = size * zz
            j = h * 4 + zz
            spans = ((0, 0, 32), (1, 0, 32), (2, 0, 16)) if p == 0 else ((2, 16, 16), (3, 0, 32))
            for yy, skip, n in spans:
                for k in range(4):
                    rows = pl.ds(pl.multiple_of(288 * k + 32 * j + skip, 16), n)
                    lhs[at_row:at_row + n, 128 * k:128 * k + 128] = ra[s, yy, rows, :]
                lhs[at_row:at_row + n, lanes] = ra[s, yy, 1152 + 32 * zz + skip:1152 + 32 * zz + skip + n, :]
                at_row += n
            if p == 1:
                lhs[at_row:at_row + 16, 0:512] = grem[rows_of(j, 16), :]
                lhs[at_row:at_row + 16, lanes] = gremf[16 * zz:16 * zz + 16, :]

    def multiply(p, s):
        if p == 0:
            arrive(gather_own(s, 1))
            for d in (0, 1, 3):
                unfold_block(s, (x + d) & 3)
            arrive(gather_relay(s))
            unfold(s)
        first, size, _ = PARTS[p]
        rows = slice(first, first + size)

        def product(h):
            gather_lhs(s, p, h)
            return nt(lhs[0:4 * size, :], rhs[...]).reshape(4, size, 1152)

        ps[s, :, rows, :] = product(1 - c).astype(BF)
        start(swap(s, p))
        pf[:, rows, :] = product(c)

    def each16(first, count, what):
        def one(i, _):
            what(pl.ds(pl.multiple_of(first + i * 16, 16), 16))
            return 0

        lax.fori_loop(0, count // 16, one, 0)

    def here_sum(s, zz, rows):
        return pf[zz, rows, :] + cx[s, zz, rows, :].astype(F32)

    def far(p, s):
        first, size, _ = PARTS[p]
        arrive(swap(s, p)[:1])

        def add(rows):
            q1[s, rows, :] = here_sum(s, (z + 2) & 3, rows).astype(BF)

        each16(first, size, add)
        start(zstep1(s, p))

    def near(p, s):
        first, size, up = PARTS[p]
        arrive(swap(s, p)[1:])
        arrive(zstep1(s, p))
        zup, zdown = ((z + step) & 3 for step in steps_of(s))

        def add_up(rows):
            q2[s, 0, rows, :] = (here_sum(s, zup, rows) + z1[s, rows, :].astype(F32)).astype(BF)
            q2[s, 1, rows, :] = here_sum(s, zdown, rows).astype(BF)

        def add_down(rows):
            q2[s, 0, rows, :] = here_sum(s, zup, rows).astype(BF)
            q2[s, 1, rows, :] = (here_sum(s, zdown, rows) + z1[s, rows, :].astype(F32)).astype(BF)

        each16(first, up, add_up)
        each16(first + up, size - up, add_down)
        start(zstep2(s, p))

        def keep(rows):
            own[s, rows, :] = here_sum(s, z, rows)

        each16(first, size, keep)

    def total(p, s):
        first, size, _ = PARTS[p]
        base = TURNED[p][0]
        arrive(zstep2(s, p))

        def add(i, _):
            rows = pl.ds(pl.multiple_of(first + 16 * i, 16), 16)
            v = own[s, rows, :] + z2[s, 0, rows, :].astype(F32) + z2[s, 1, rows, :].astype(F32)
            v = v.astype(BF)
            db[s, rows, :] = v
            for xx in range(4):
                for k in range(2):
                    to = pl.ds(pl.multiple_of(base + size * k + 16 * i, 16), 16)
                    dx[s, xx, to, :] = v[:, 256 * xx + 128 * k:256 * xx + 128 * k + 128]
            return 0

        lax.fori_loop(0, size // 16, add, 0)
        if p == 1:
            tail = db[s, :, 1024:1152].astype(F32)
            for xx in range(4):
                lanes = slice(32 * xx, 32 * xx + 32)
                packed = [tail[48 * g:48 * g + 48, lanes] for g in range(3)]
                packed.append(jnp.zeros((48, 32), F32))
                dx[s, xx, 288:336, :] = jnp.concatenate(packed, axis=1).astype(BF)
        start(turn_copies(s, p))
        span = slice(base, base + TURNED[p][1])
        txm[s, x, span, :] = dx[s, x, span, :]
        if p == 1:
            for yy in range(4):
                for k in range(9):
                    hx[s, yy, 32 * k:32 * k + 32, :] = db[s, 32 * yy:32 * yy + 32, 128 * k:128 * k + 128]
                mine = db[s, 128:144, :].astype(F32)[4 * yy:4 * yy + 4]
                for k in range(3):
                    lanes = [128 * k + 256 * xx if k < 2 else 1024 for xx in range(4)]
                    hx[s, yy, 288 + 16 * k:304 + 16 * k, :] = jnp.concatenate(
                        [mine[:, i:i + 128] for i in lanes], axis=0
                    ).astype(BF)
            start(here_copies(s))
            hm[s, y] = hx[s, y]

    def turn(s):
        for p in range(2):
            arrive(turn_copies(s, p))
        for xx in range(4):
            packed = txm[s, xx, 288:336, :]
            groups = [packed * mk[8 + g:9 + g, 0:128] for g in range(3)]
            at_row = 128 * xx
            for k in range(2):
                lanes = slice(128 * k, 128 * k + 128)
                wm[at_row:at_row + 80, lanes] = txm[s, xx, 80 * k:80 * k + 80, :]
                wm[at_row + 80:at_row + 128, lanes] = txm[s, xx, 160 + 64 * k:208 + 64 * k, :]
                wr[64 + 16 * xx:80 + 16 * xx, lanes] = txm[s, xx, 208 + 64 * k:224 + 64 * k, :]
            wm[at_row:at_row + 48, 256:384] = groups[0]
            wm[at_row + 48:at_row + 96, 256:384] = groups[1]
            wm[at_row + 96:at_row + 128, 256:384] = groups[2][0:32]
            wr[64 + 16 * xx:80 + 16 * xx, 256:384] = groups[2][32:48]
        main = nt(sel_m[...], wm[...]).astype(BF)
        rest = jnp.zeros((128, 128), F32)
        for xx in range(4):
            um[s, :, 32 * xx:32 * xx + 32, :] = main[:, 128 * xx:128 * xx + 128].reshape(8, 32, 128)
            rest += nt(sel_x[xx], wm[128 * xx:128 * xx + 128, :])
        um[s, :, 128:144, :] = rest.astype(BF).reshape(8, 16, 128)
        low, high = wr[64:192, :], wr[0:128, :]
        rest = nt(sel_a[0], low) + nt(sel_a[1], high)
        um[s, :, 144:160, :] = rest.astype(BF).reshape(8, 16, 128)
        every = sel_x[0] + sel_x[1] + sel_x[2] + sel_x[3]
        rest = nt(every, low)
        keep = ((iota((128, 128), 1) >> 4) & 3) == ((iota((128, 128), 0) >> 2) & 3)
        um[s, :, 160:176, :] = jnp.where(keep, rest, 0.0).astype(BF).reshape(8, 16, 128)
        start(last_copies(s))
        tm[s, jme] = um[s, jme]

    def here(s):
        arrive(here_copies(s))
        slot = s & 1
        dev = row * 8 + col
        row_limit = l_ref[s, dev >> 4] - (dev & 15) * 36
        row_live = (iota((36, 1), 0) < row_limit).astype(F32)
        row_energy = er[s, 0:36, 0:1]
        lane = iota((1, 1152), 1)
        tiles = [[hm[s, yy, 32 * k:32 * k + 32, :].astype(F32) for k in range(9)] for yy in range(4)]
        rests = [[hm[s, yy, 288 + 16 * k:304 + 16 * k, :].astype(F32) for k in range(3)] for yy in range(4)]
        for xx in range(4):
            top, low = [], []
            for yy in range(4):
                last = slice(32 * xx, 32 * xx + 32)
                top += [tiles[yy][2 * xx], tiles[yy][2 * xx + 1], tiles[yy][8][:, last]]
                low += [v[4 * xx:4 * xx + 4] for v in rests[yy][:2]] + [rests[yy][2][4 * xx:4 * xx + 4, last]]
            cols = slice(1152 * xx, 1152 * xx + 1152)
            ob[s, 0:32, cols] = jnp.concatenate(top, axis=1)
            ob[s, 32:36, cols] = jnp.concatenate(low, axis=1)
            bound = jnp.where(lane < 576, l_ref[s, 2 * xx], l_ref[s, 2 * xx + 1] + 576)
            col_live = (lane < bound).astype(F32)
            sc[slot, :, cols] = row_live * col_live / (row_energy + e_ref[pl.ds(s, 1), cols])

    def done(s):
        slot = s & 1
        arrive(last_copies(s))

        def across(a, b):
            return jnp.concatenate([tm[s, j, a:b, :] for j in range(8)], axis=1)

        first = across(0, 144)
        packed = across(144, 160)
        second = jnp.concatenate([packed * mk[i:i + 1, :] for i in range(8)] + [across(160, 176)], axis=0)
        got = nn(jnp.concatenate([first, second], axis=1), s12[...])
        for xx in range(4):
            cols = slice(1152 * xx, 1152 * xx + 1152)
            ob[s, 0:32, cols] = (ob[s, 0:32, cols] + got[32 * xx:32 * xx + 32]) * sc[slot, 0:32, cols]
            ob[s, 32:36, cols] = (ob[s, 32:36, cols] + got[128 + 4 * xx:132 + 4 * xx]) * sc[slot, 32:36, cols]
            result_copy(s, xx).start()

    def early_constants():
        i = iota((288, 288), 0)
        k = iota((288, 288), 1)
        head = 36 * natural(i >> 5) + (i & 31)
        tail = 36 * natural((i - 256) >> 2) + 32 + (i & 3)
        pm[...] = ones_where(k == jnp.where(i < 256, head, tail))

    def late_constants():
        i = iota((128, 128), 0)
        k = iota((128, 128), 1)
        qp[...] = ones_where(k == 32 * ((i >> 2) & 3) + 4 * (i >> 4) + (i & 3))
        i = iota((64, 64), 0)
        k = iota((64, 64), 1)
        fold[...] = ones_where(k == 16 * ((i >> 2) & 3) + 4 * (i >> 4) + (i & 3))
        i = iota((128, 512), 0)
        k = iota((128, 512), 1)
        lane = k & 127
        half = k >> 8
        hit = ((i >> 6) == half) & ((lane & 63) == (i & 63)) & ((lane >> 6) == ((k >> 7) & 1))
        ue[...] = ones_where(hit)

        def select(q, k):
            return (k == q) | ((k >= 256) & (k < 352) & (((k - 256) & 31) == q - 256))

        def shape3(n):
            return tuple(iota((8, n, 384), d) for d in range(3))

        j, t, k = shape3(32)
        sel_m[...] = ones_where(select(36 * natural(j) + t, k)).reshape(256, 384)
        j, t, k = shape3(16)
        for xx in range(4):
            hit = select(36 * natural(j) + 32 + (t & 3), k) & ((t >> 2) == xx)
            sel_x[xx] = ones_where(hit).reshape(128, 384)
        for h in range(2):
            sel_a[h] = ones_where(select(36 * natural(j) + 16 * h + t, k)).reshape(128, 384)
        wr[...] = jnp.zeros(wr.shape, BF)

        def fill(j, _):
            rows = rows_of(j, 128)
            r = iota((128, 1152), 0)
            k = iota((128, 1152), 1)
            base = 36 * natural(j)
            s12[rows, :] = ones_where(k == 288 * (r >> 5) + base + (r & 31))
            rows = pl.ds(pl.multiple_of(128 * j + 1024, 128), 128)
            s12[rows, :] = ones_where(k == 288 * ((r >> 2) & 3) + base + 32 + (r & 3))
            return 0

        lax.fori_loop(0, 8, fill, 0)
        r = iota((16, 1024), 0)
        k = iota((16, 1024), 1)
        lane = k & 127
        quarter = ((lane >> 4) & 3) * 2 + (lane >> 6)
        mk[...] = ones_where(((r < 8) & (quarter == r)) | ((r >= 8) & ((lane >> 5) == r - 8)))
        dev = row * 8 + col
        pick = iota((40, 4608), 1) == iota((40, 4608), 0) + dev * 36
        for s in range(4):
            got = jnp.sum(jnp.where(pick, e_ref[s:s + 1, :], 0.0), axis=1, keepdims=True)
            er[s] = jnp.broadcast_to(got, (40, 128))

    early_constants()
    ready(0)
    for s in range(1, 4):
        for cp in load(s):
            cp.start()
    pl.semaphore_wait(barrier, len(partners))
    start(gather_own(0, 0))
    start(gather_own(0, 1))
    ready(1)
    late_constants()

    def drain(s):
        copies = gather_own(s, 0) + gather_own(s, 1) + gather_relay(s) + here_copies(s)
        for p in range(2):
            copies += swap(s, p) + zstep1(s, p) + zstep2(s, p) + turn_copies(s, p)
        for cp in copies:
            cp.wait_send()

        @pl.when(s < 3)
        def _():
            for cp in last_copies(s):
                cp.wait_send()

    work = {
        "ready": ready, "relay": relay, "turn": turn, "here": here, "done": done, "drain": drain,
        "mul0": functools.partial(multiply, 0), "mul1": functools.partial(multiply, 1),
        "far0": functools.partial(far, 0), "far1": functools.partial(far, 1),
        "near0": functools.partial(near, 0), "near1": functools.partial(near, 1),
        "sum0": functools.partial(total, 0), "sum1": functools.partial(total, 1),
    }
    steps = ORDER[1:]

    def one_step(i, _):
        for name, what in work.items():
            places = [(at_step, s) for at_step, (n, s) in enumerate(steps) if n == name]
            now = functools.reduce(jnp.logical_or, [i == at_step for at_step, _ in places])
            s = sum(jnp.where(i == at_step, s, 0) for at_step, s in places)
            pl.when(now)(functools.partial(what, s))
        return 0

    lax.fori_loop(0, len(steps), one_step, 0)

    for cp in last_copies(3):
        cp.wait_send()
    for s in range(4):
        for xx in range(4):
            result_copy(s, xx).wait()


def body(amplitudes, integrals, pair_energy, block_len):
    bf = lambda *shape: pltpu.VMEM(shape, BF)
    f32 = lambda *shape: pltpu.VMEM(shape, F32)
    dma = lambda *shape: pltpu.SemaphoreType.DMA(shape)
    scratch = [
        bf(4, 288, 576), bf(4, 288, 576),
        bf(4, 4, 1296, 128), bf(4, 4, 1296, 128),
        bf(1152, 768), bf(128, 512), bf(64, 128), bf(320, 768),
        bf(4, 4, 144, 1152), bf(4, 4, 144, 1152), f32(4, 144, 1152),
        bf(4, 144, 1152), bf(4, 2, 144, 1152), bf(4, 144, 1152), bf(4, 2, 144, 1152),
        f32(4, 144, 1152), bf(4, 144, 1152), bf(4, 4, 336, 128),
        bf(4, 4, 336, 128), bf(4, 4, 336, 128), bf(4, 4, 336, 128),
        bf(512, 384), bf(192, 384), bf(4, 8, 176, 128), bf(4, 8, 176, 128), f32(2, 36, 4608),
        bf(288, 288), bf(128, 128), bf(128, 512), bf(64, 64),
        bf(256, 384), bf(4, 128, 384), bf(2, 128, 384),
        bf(2048, 1152), bf(16, 1024), f32(4, 40, 128), f32(4, 36, 4608),
        dma(4, 2), dma(4, 2, 2, 2), dma(4, 2, 2, 2), dma(4, 2, 2), dma(4, 2, 2), dma(4, 2, 4), dma(4, 2, 4),
        dma(4, 2, 2), dma(4, 2, 2), dma(4, 2, 2), dma(4, 2, 2),
        dma(4, 3), dma(4, 3), dma(4, 3, 2), dma(4, 3, 2), dma(4, 7), dma(4, 7), dma(4, 4),
    ]
    count, npairs = pair_energy.shape
    turned = pl.pallas_call(
        kernel,
        out_shape=pltpu.VMEM((npairs // 128, count, npairs), F32),
        in_specs=[
            pl.BlockSpec(memory_space=pl.ANY),
            pl.BlockSpec(memory_space=pl.ANY),
            pl.BlockSpec(memory_space=pltpu.VMEM),
            pl.BlockSpec(memory_space=pltpu.SMEM),
        ],
        out_specs=pl.BlockSpec(memory_space=pltpu.VMEM),
        scratch_shapes=scratch,
        compiler_params=pltpu.CompilerParams(
            collective_id=0, has_side_effects=True, vmem_limit_bytes=60 << 20
        ),
        name="cycle",
    )(amplitudes, jnp.swapaxes(integrals, 1, 2), pair_energy, block_len)
    return jnp.swapaxes(turned, 0, 1)


def solution(mesh):
    return jax.shard_map(
        body,
        mesh=mesh,
        in_specs=(P(None, "row", "col"), P(None, "col", "row"), P(), P()),
        out_specs=P(None, ("row", "col"), None),
        check_vma=False,
    )
```

```python
import functools

import jax
import jax.numpy as jnp
from jax import lax
from jax.experimental import pallas as pl
from jax.experimental.pallas import tpu as pltpu
from jax.sharding import PartitionSpec as P

MESH = pl.DeviceIdType.MESH
BF = jnp.bfloat16
F32 = jnp.float32
I32 = jnp.int32

PARTS = ((0, 96, 48, 0, 768), (0, 96, 48, 768, 384), (96, 48, 32, 0, 1152))
SLOT = {1: 1, 3: 2, 2: 3}
PIECES = ((0, 656), (656, 640))

TURNED = ((0, 192), (192, 144))

ORDER = (
    ("ready", 1), ("relay", 0), ("ready", 2), ("mul0", 0), ("far0", 0), ("mul1", 0), ("far1", 0), ("near0", 0),
    ("mul2", 0), ("relay", 1), ("near1", 0), ("far2", 0), ("mul0", 1), ("far0", 1), ("near2", 0), ("mul1", 1),
    ("far1", 1), ("ready", 3), ("near0", 1), ("mul2", 1), ("relay", 2), ("far2", 1), ("near1", 1), ("mul0", 2),
    ("far0", 2), ("near2", 1), ("mul1", 2), ("far1", 2), ("near0", 2), ("relay", 3), ("mul2", 2), ("far2", 2),
    ("sum0", 1), ("near1", 2), ("mul0", 3), ("far0", 3), ("sum0", 0), ("near2", 2), ("mul1", 3), ("sum1", 0),
    ("far1", 3), ("sum1", 1), ("sum2", 0), ("near0", 3), ("mul2", 3), ("sum2", 1), ("far2", 3), ("near1", 3),
    ("turn", 0), ("sum0", 2), ("sum1", 2), ("drain", 0), ("near2", 3), ("sum2", 2), ("turn", 1), ("here", 1),
    ("sum0", 3), ("here", 0), ("sum1", 3), ("done", 0), ("turn", 2), ("sum2", 3), ("turn", 3), ("here", 2),
    ("drain", 3), ("done", 1), ("here", 3), ("done", 2), ("drain", 2), ("drain", 1), ("done", 3),
)


def nt(a, b):
    return lax.dot_general(a, b, (((1,), (1,)), ((), ())), preferred_element_type=F32)


def nn(a, b):
    return jnp.dot(a, b, preferred_element_type=F32)


def iota(shape, dim):
    return lax.broadcasted_iota(I32, shape, dim)


def natural(j):
    return 2 * (j & 3) + (j >> 2)


def ones_where(hit):
    return hit.astype(F32).astype(BF)


def kernel(
    a_hbm, b_hbm, e_ref, l_ref, o_ref,
    av, bv, ra, rb, rhs, grem, gremf, lhs, ps, cx, pf, q1, q2, z1, z2, own, db, dx, hx, hm, txm,
    wm, wr, um, tm, sc, pm, qp, ue, fold, sel_m, sel_x, sel_a, s12, mk, er, ob,
    lsem, gos, gor, grs, grr, cs, cr, z1s, z1r, z2s, z2r, hs, hrr, xs, xr, ts, tsr, osem,
):
    row = lax.axis_index("row")
    col = lax.axis_index("col")
    x, y = row >> 2, row & 3
    z, c = col >> 1, col & 1
    jme = c * 4 + z

    def at(dx, dy, dz, dc):
        return (((x + dx) & 3) * 4 + ((y + dy) & 3), ((z + dz) & 3) * 2 + ((c + dc) & 1))

    def remote(src, dst, ssem, rsem, where):
        return pltpu.make_async_remote_copy(
            src_ref=src, dst_ref=dst, send_sem=ssem, recv_sem=rsem, device_id=where, device_id_type=MESH
        )

    def load(s):
        return (
            pltpu.make_async_copy(a_hbm.at[s], av.at[s], lsem.at[s, 0]),
            pltpu.make_async_copy(b_hbm.at[s], bv.at[s], lsem.at[s, 1]),
        )

    for cp in load(0):
        cp.start()

    barrier = pltpu.get_barrier_semaphore()
    partners = [at(d, 0, 0, 0) for d in (1, 2, 3)] + [at(0, d, 0, 0) for d in (1, 2, 3)]
    partners += [at(0, 0, i // 2, i % 2) for i in range(1, 8)]
    for p in partners:
        pl.semaphore_signal(barrier, 1, device_id=p, device_id_type=MESH)

    def rows_of(v, size):
        return pl.ds(pl.multiple_of(v * size, size), size)

    def gather_own(s, which):
        out = []
        for d, step in ((0, 1), (1, 3)):
            first, size = PIECES[d ^ which]
            rows = pl.ds(first, size)
            blk = ra.at[s, y, rows, :]
            out.append(remote(blk, blk, gos.at[s, d, which, 0], gor.at[s, d, which, 0], at(0, step, 0, 0)))
            blk = rb.at[s, x, rows, :]
            out.append(remote(blk, blk, gos.at[s, d, which, 1], gor.at[s, d, which, 1], at(step, 0, 0, 0)))
        return out

    def gather_relay(s):
        out = []
        for d, step in ((0, 1), (1, 3)):
            first, size = PIECES[d]
            rows = pl.ds(first, size)
            blk = ra.at[s, (y + 4 - step) & 3, rows, :]
            out.append(remote(blk, blk, grs.at[s, d, 0], grr.at[s, d, 0], at(0, step, 0, 0)))
            blk = rb.at[s, (x + 4 - step) & 3, rows, :]
            out.append(remote(blk, blk, grs.at[s, d, 1], grr.at[s, d, 1], at(step, 0, 0, 0)))
        return out

    def spans(p):
        first, size, _, lane, width = PARTS[p]
        return pl.ds(first, size), pl.ds(lane, width)

    def swap(s, p):
        rows, lanes = spans(p)
        out = []
        for i, step in enumerate((2, 1, 3, 0)):
            zz = (z + step) & 3
            out.append(remote(
                ps.at[s, zz, rows, lanes], cx.at[s, zz, rows, lanes], cs.at[s, p, i], cr.at[s, p, i], at(0, 0, 0, 1)
            ))
        return out

    def steps_of(s):
        odd = s & 1
        return 1 + 2 * odd, 3 - 2 * odd

    def zstep1(s, p):
        first, size, up, _, _ = PARTS[p]
        lanes = spans(p)[1]
        out = []
        for d, step, rows in zip((0, 1), steps_of(s), (pl.ds(first, up), pl.ds(first + up, size - up))):
            out.append(remote(
                q1.at[s, rows, lanes], z1.at[s, rows, lanes], z1s.at[s, p, d], z1r.at[s, p, d], at(0, 0, step, 0)
            ))
        return out

    def zstep2(s, p):
        rows, lanes = spans(p)
        return [
            remote(
                q2.at[s, d, rows, lanes], z2.at[s, d, rows, lanes],
                z2s.at[s, p, d], z2r.at[s, p, d], at(0, 0, step, 0),
            )
            for d, step in zip((0, 1), steps_of(s))
        ]

    def here_copies(s):
        return [
            remote(hx.at[s, (y + d) & 3], hm.at[s, y], hs.at[s, d - 1], hrr.at[s, d - 1], at(0, d, 0, 0))
            for d in (1, 2, 3)
        ]

    def turn_copies(s, piece, targets=(1, 3, 2)):
        rows = pl.ds(*TURNED[piece])
        return [
            remote(
                dx.at[s, SLOT[d], rows, :], txm.at[s, x, rows, :],
                xs.at[s, d - 1, piece], xr.at[s, d - 1, piece], at(d, 0, 0, 0),
            )
            for d in targets
        ]

    def last_copies(s):
        out = []
        for i in (2, 6, 4, 3, 7, 5, 1):
            dz, dc = i // 2, i % 2
            jto = ((c + dc) & 1) * 4 + ((z + dz) & 3)
            out.append(remote(
                um.at[s, jto], tm.at[s, jme], ts.at[s, i - 1], tsr.at[s, i - 1], at(0, 0, dz, dc)
            ))
        return out

    def result_copy(s, xx):
        cols = pl.ds(1152 * xx, 1152)
        return pltpu.make_async_copy(ob.at[s, :, cols], o_ref.at[:, s, cols], osem.at[s, xx])

    def start(copies):
        for cp in copies:
            cp.start()

    def arrive(copies):
        for cp in copies:
            cp.wait_recv()

    def fold_lanes(low, high):
        return jnp.concatenate([low, high], axis=1)

    def ready(s):
        for cp in load(s):
            cp.wait()
        limit = l_ref[s, col]
        masked = jnp.where(iota((288, 576), 1) < limit, av[s].astype(F32), 0.0).astype(BF)
        turned = nn(pm[...], masked)
        b = bv[s]
        for k in range(4):
            ra[s, y, 288 * k:288 * k + 288, :] = turned[:, 128 * k:128 * k + 128].astype(BF)
            rb[s, x, 288 * k:288 * k + 288, :] = b[:, 128 * k:128 * k + 128]
        rest = turned[:, 512:576]
        ra[s, y, 1152:1280, :] = fold_lanes(rest[0:128], rest[128:256]).astype(BF)
        ra[s, y, 1280:1296, :] = fold_lanes(rest[256:272], rest[272:288]).astype(BF)
        rest = b[:, 512:576].astype(F32)
        rb[s, x, 1152:1296, :] = fold_lanes(rest[0:144], rest[144:288]).astype(BF)

    def relay(s):
        arrive(gather_own(s, 0))
        start(gather_relay(s))

        @pl.when(s < 3)
        def _():
            start(gather_own(s + 1, 0))
            start(gather_own(s + 1, 1))

    def near_to(v, slot):
        return (v + (slot ^ (slot >> 1))) & 3

    def unfold(s, slot):
        xx = near_to(x, slot)
        got = nn(rb[s, xx, 1152:1296, :], ue[...]).astype(BF)
        low, high = got[:, 0:256], got[:, 256:512]
        main, rest = 256 * slot, slice(1024 + 32 * slot, 1056 + 32 * slot)
        for k in range(4):
            lanes = slice(128 * k, 128 * k + 128)
            rhs[main:main + 256, lanes] = rb[s, xx, 288 * k:288 * k + 256, :]
            rhs[rest, lanes] = rb[s, xx, 288 * k + 256:288 * k + 288, :]
        rhs[main:main + 144, 512:768] = low
        rhs[main + 144:main + 256, 512:768] = high[0:112]
        rhs[rest, 512:768] = high[112:144]

    def last_rows(s):
        for k in range(4):
            grem[:, 128 * k:128 * k + 128] = nn(
                qp[...], ra[s, :, 288 * k + 256:288 * k + 288, :].reshape(128, 128)
            ).astype(BF)
        gremf[...] = nn(fold[...], ra[s, :, 1280:1296, :].reshape(64, 128)).astype(BF)

    def gather_lhs(s, slots, h, i):
        lanes = pl.ds(pl.multiple_of(512 + 128 * h, 128), 128)
        lhs[i, :, pl.ds(pl.multiple_of(640 - 128 * h, 128), 128)] = jnp.zeros((384, 128), BF)
        at_row = 0
        for zz in range(4):
            j = h * 4 + zz
            for slot in slots:
                yy = near_to(y, slot)
                for k in range(4):
                    rows = pl.ds(pl.multiple_of(288 * k + 32 * j, 16), 32)
                    lhs[i, at_row:at_row + 32, 128 * k:128 * k + 128] = ra[s, yy, rows, :]
                lhs[i, at_row:at_row + 32, lanes] = ra[s, yy, 1152 + 32 * zz:1184 + 32 * zz, :]
                at_row += 32
            if slots == (3,):
                lhs[i, at_row:at_row + 16, 0:512] = grem[rows_of(j, 16), :]
                lhs[i, at_row:at_row + 16, lanes] = gremf[16 * zz:16 * zz + 16, :]
                at_row += 16

    def multiply(p, s):
        if p == 0:
            arrive(gather_own(s, 1))
            for slot in range(3):
                unfold(s, slot)
            for i, h in ((0, 1 - c), (1, c)):
                gather_lhs(s, (0, 1, 2), h, i)
        if p == 1:
            arrive(gather_relay(s))
            unfold(s, 3)
        if p == 2:
            last_rows(s)
            for i, h in ((0, 1 - c), (1, c)):
                gather_lhs(s, (3,), h, i)
        first, size, _, lane, width = PARTS[p]
        rows, lanes = slice(first, first + size), slice(lane, lane + width)

        def product(i):
            return nt(lhs[i, 0:4 * size, :], rhs[lanes, :]).reshape(4, size, width)

        ps[s, :, rows, lanes] = product(0).astype(BF)
        start(swap(s, p))
        pf[:, rows, lanes] = product(1)

    def each16(first, count, what):
        def one(i, _):
            what(pl.ds(pl.multiple_of(first + i * 16, 16), 16))
            return 0

        lax.fori_loop(0, count // 16, one, 0)

    def here_sum(s, zz, rows, lanes):
        return pf[zz, rows, lanes] + cx[s, zz, rows, lanes].astype(F32)

    def far(p, s):
        first, size, _, lane, width = PARTS[p]
        lanes = slice(lane, lane + width)
        arrive(swap(s, p)[:1])

        def add(rows):
            q1[s, rows, lanes] = here_sum(s, (z + 2) & 3, rows, lanes).astype(BF)

        each16(first, size, add)
        start(zstep1(s, p))

    def near(p, s):
        first, size, up, lane, width = PARTS[p]
        lanes = slice(lane, lane + width)
        arrive(swap(s, p)[1:])
        arrive(zstep1(s, p))
        zup, zdown = ((z + step) & 3 for step in steps_of(s))

        def add_up(rows):
            q2[s, 0, rows, lanes] = (here_sum(s, zup, rows, lanes) + z1[s, rows, lanes].astype(F32)).astype(BF)
            q2[s, 1, rows, lanes] = here_sum(s, zdown, rows, lanes).astype(BF)

        def add_down(rows):
            q2[s, 0, rows, lanes] = here_sum(s, zup, rows, lanes).astype(BF)
            q2[s, 1, rows, lanes] = (here_sum(s, zdown, rows, lanes) + z1[s, rows, lanes].astype(F32)).astype(BF)

        each16(first, up, add_up)
        each16(first + up, size - up, add_down)
        start(zstep2(s, p))

        def keep(rows):
            own[s, rows, lanes] = here_sum(s, z, rows, lanes)

        each16(first, size, keep)

    def total(p, s):
        first, size, _, lane, width = PARTS[p]
        lanes = slice(lane, lane + width)
        base = 0 if p < 2 else TURNED[1][0]
        slots = ((0, 1, 2), (3,), (0, 1, 2, 3))[p]
        arrive(zstep2(s, p))

        def add(i, _):
            rows = pl.ds(pl.multiple_of(first + 16 * i, 16), 16)
            v = own[s, rows, lanes] + z2[s, 0, rows, lanes].astype(F32) + z2[s, 1, rows, lanes].astype(F32)
            v = v.astype(BF)
            db[s, rows, lanes] = v
            for slot in slots:
                for k in range(2):
                    to = pl.ds(pl.multiple_of(base + size * k + 16 * i, 16), 16)
                    at_lane = 256 * slot + 128 * k - lane
                    dx[s, slot, to, :] = v[:, at_lane:at_lane + 128]
            return 0

        lax.fori_loop(0, size // 16, add, 0)
        if p == 0:
            start(turn_copies(s, 0, (1, 3)))
            txm[s, x, 0:192, :] = dx[s, 0, 0:192, :]
        if p == 1:
            start(turn_copies(s, 0, (2,)))
        if p == 2:
            tail = db[s, :, 1024:1152].astype(F32)
            for slot in range(4):
                cut = slice(32 * slot, 32 * slot + 32)
                packed = [tail[48 * g:48 * g + 48, cut] for g in range(3)]
                packed.append(jnp.zeros((48, 32), F32))
                dx[s, slot, 288:336, :] = jnp.concatenate(packed, axis=1).astype(BF)
            start(turn_copies(s, 1))
            txm[s, x, 192:336, :] = dx[s, 0, 192:336, :]
            low = db[s, 128:144, :].astype(F32)
            for yy in range(4):
                mine = low[4 * yy:4 * yy + 4]
                for k in range(3):
                    at_lanes = [128 * k + 256 * slot if k < 2 else 1024 for slot in range(4)]
                    hx[s, yy, 288 + 16 * k:304 + 16 * k, :] = jnp.concatenate(
                        [mine[:, i:i + 128] for i in at_lanes], axis=0
                    ).astype(BF)
            for slot in range(4):
                for k in range(9):
                    hx[s, near_to(y, slot), 32 * k:32 * k + 32, :] = db[
                        s, 32 * slot:32 * slot + 32, 128 * k:128 * k + 128
                    ]
            start(here_copies(s))
            hm[s, y] = hx[s, y]

    def turn(s):
        for p in range(2):
            arrive(turn_copies(s, p))
        for xx in range(4):
            packed = txm[s, xx, 288:336, :]
            groups = [packed * mk[8 + g:9 + g, 0:128] for g in range(3)]
            at_row = 128 * xx
            for k in range(2):
                lanes = slice(128 * k, 128 * k + 128)
                wm[at_row:at_row + 96, lanes] = txm[s, xx, 96 * k:96 * k + 96, :]
                wm[at_row + 96:at_row + 128, lanes] = txm[s, xx, 192 + 48 * k:224 + 48 * k, :]
                wr[64 + 16 * xx:80 + 16 * xx, lanes] = txm[s, xx, 224 + 48 * k:240 + 48 * k, :]
            wm[at_row:at_row + 48, 256:384] = groups[0]
            wm[at_row + 48:at_row + 96, 256:384] = groups[1]
            wm[at_row + 96:at_row + 128, 256:384] = groups[2][0:32]
            wr[64 + 16 * xx:80 + 16 * xx, 256:384] = groups[2][32:48]
        main = nt(sel_m[...], wm[...]).astype(BF)
        rest = jnp.zeros((128, 128), F32)
        for xx in range(4):
            um[s, :, 32 * xx:32 * xx + 32, :] = main[:, 128 * xx:128 * xx + 128].reshape(8, 32, 128)
            rest += nt(sel_x[xx], wm[128 * xx:128 * xx + 128, :])
        um[s, :, 128:144, :] = rest.astype(BF).reshape(8, 16, 128)
        low, high = wr[64:192, :], wr[0:128, :]
        rest = nt(sel_a[0], low) + nt(sel_a[1], high)
        um[s, :, 144:160, :] = rest.astype(BF).reshape(8, 16, 128)
        every = sel_x[0] + sel_x[1] + sel_x[2] + sel_x[3]
        rest = nt(every, low)
        keep = ((iota((128, 128), 1) >> 4) & 3) == ((iota((128, 128), 0) >> 2) & 3)
        um[s, :, 160:176, :] = jnp.where(keep, rest, 0.0).astype(BF).reshape(8, 16, 128)
        start(last_copies(s))
        tm[s, jme] = um[s, jme]

    def here(s):
        arrive(here_copies(s))
        slot = s & 1
        dev = row * 8 + col
        row_limit = l_ref[s, dev >> 4] - (dev & 15) * 36
        row_live = (iota((36, 1), 0) < row_limit).astype(F32)
        row_energy = er[s, 0:36, 0:1]
        lane = iota((1, 1152), 1)
        tiles = [[hm[s, yy, 32 * k:32 * k + 32, :].astype(F32) for k in range(9)] for yy in range(4)]
        rests = [[hm[s, yy, 288 + 16 * k:304 + 16 * k, :].astype(F32) for k in range(3)] for yy in range(4)]
        for xx in range(4):
            top, low = [], []
            for yy in range(4):
                last = slice(32 * xx, 32 * xx + 32)
                top += [tiles[yy][2 * xx], tiles[yy][2 * xx + 1], tiles[yy][8][:, last]]
                low += [v[4 * xx:4 * xx + 4] for v in rests[yy][:2]] + [rests[yy][2][4 * xx:4 * xx + 4, last]]
            xto = near_to(x, xx)
            cols = pl.ds(pl.multiple_of(1152 * xto, 1152), 1152)
            ob[s, 0:32, cols] = jnp.concatenate(top, axis=1)
            ob[s, 32:36, cols] = jnp.concatenate(low, axis=1)
            bound = jnp.where(lane < 576, l_ref[s, 2 * xto], l_ref[s, 2 * xto + 1] + 576)
            col_live = (lane < bound).astype(F32)
            sc[slot, :, cols] = row_live * col_live / (row_energy + e_ref[pl.ds(s, 1), cols])

    def done(s):
        slot = s & 1
        arrive(last_copies(s))

        def across(a, b):
            return jnp.concatenate([tm[s, j, a:b, :] for j in range(8)], axis=1)

        first = across(0, 144)
        packed = across(144, 160)
        second = jnp.concatenate([packed * mk[i:i + 1, :] for i in range(8)] + [across(160, 176)], axis=0)
        got = nn(jnp.concatenate([first, second], axis=1), s12[...])
        for xx in range(4):
            cols = slice(1152 * xx, 1152 * xx + 1152)
            ob[s, 0:32, cols] = (ob[s, 0:32, cols] + got[32 * xx:32 * xx + 32]) * sc[slot, 0:32, cols]
            ob[s, 32:36, cols] = (ob[s, 32:36, cols] + got[128 + 4 * xx:132 + 4 * xx]) * sc[slot, 32:36, cols]
            result_copy(s, xx).start()

    def early_constants():
        i = iota((288, 288), 0)
        k = iota((288, 288), 1)
        head = 36 * natural(i >> 5) + (i & 31)
        tail = 36 * natural((i - 256) >> 2) + 32 + (i & 3)
        pm[...] = ones_where(k == jnp.where(i < 256, head, tail))

    def late_constants():
        i = iota((128, 128), 0)
        k = iota((128, 128), 1)
        qp[...] = ones_where(k == 32 * ((i >> 2) & 3) + 4 * (i >> 4) + (i & 3))
        i = iota((64, 64), 0)
        k = iota((64, 64), 1)
        fold[...] = ones_where(k == 16 * ((i >> 2) & 3) + 4 * (i >> 4) + (i & 3))
        i = iota((128, 512), 0)
        k = iota((128, 512), 1)
        lane = k & 127
        half = k >> 8
        hit = ((i >> 6) == half) & ((lane & 63) == (i & 63)) & ((lane >> 6) == ((k >> 7) & 1))
        ue[...] = ones_where(hit)

        def select(q, k):
            return (k == q) | ((k >= 256) & (k < 352) & (((k - 256) & 31) == q - 256))

        def shape3(n):
            return tuple(iota((8, n, 384), d) for d in range(3))

        j, t, k = shape3(32)
        sel_m[...] = ones_where(select(36 * natural(j) + t, k)).reshape(256, 384)
        j, t, k = shape3(16)
        for xx in range(4):
            hit = select(36 * natural(j) + 32 + (t & 3), k) & ((t >> 2) == xx)
            sel_x[xx] = ones_where(hit).reshape(128, 384)
        for h in range(2):
            sel_a[h] = ones_where(select(36 * natural(j) + 16 * h + t, k)).reshape(128, 384)
        wr[...] = jnp.zeros(wr.shape, BF)

        def fill(j, _):
            rows = rows_of(j, 128)
            r = iota((128, 1152), 0)
            k = iota((128, 1152), 1)
            base = 36 * natural(j)
            s12[rows, :] = ones_where(k == 288 * near_to(y, r >> 5) + base + (r & 31))
            rows = pl.ds(pl.multiple_of(128 * j + 1024, 128), 128)
            s12[rows, :] = ones_where(k == 288 * ((r >> 2) & 3) + base + 32 + (r & 3))
            return 0

        lax.fori_loop(0, 8, fill, 0)
        r = iota((16, 1024), 0)
        k = iota((16, 1024), 1)
        lane = k & 127
        quarter = ((lane >> 4) & 3) * 2 + (lane >> 6)
        mk[...] = ones_where(((r < 8) & (quarter == r)) | ((r >= 8) & ((lane >> 5) == r - 8)))
        dev = row * 8 + col
        pick = iota((40, 4608), 1) == iota((40, 4608), 0) + dev * 36
        for s in range(4):
            got = jnp.sum(jnp.where(pick, e_ref[s:s + 1, :], 0.0), axis=1, keepdims=True)
            er[s] = jnp.broadcast_to(got, (40, 128))

    early_constants()
    ready(0)
    for s in range(1, 4):
        for cp in load(s):
            cp.start()
    pl.semaphore_wait(barrier, len(partners))
    start(gather_own(0, 0))
    start(gather_own(0, 1))
    ready(1)
    late_constants()

    def drain(s):
        copies = gather_own(s, 0) + gather_own(s, 1) + gather_relay(s) + here_copies(s)
        for p in range(2):
            copies += turn_copies(s, p)
        for p in range(3):
            copies += swap(s, p) + zstep1(s, p) + zstep2(s, p)
        for cp in copies:
            cp.wait_send()

        @pl.when(s < 3)
        def _():
            for cp in last_copies(s):
                cp.wait_send()

    work = {
        "ready": ready, "relay": relay, "turn": turn, "here": here, "done": done, "drain": drain,
    }
    for p in range(3):
        for name, what in (("mul", multiply), ("far", far), ("near", near), ("sum", total)):
            work[name + str(p)] = functools.partial(what, p)
    steps = ORDER[1:]

    def one_step(i, _):
        for name, what in work.items():
            places = [(at_step, s) for at_step, (n, s) in enumerate(steps) if n == name]
            now = functools.reduce(jnp.logical_or, [i == at_step for at_step, _ in places])
            s = sum(jnp.where(i == at_step, s, 0) for at_step, s in places)
            pl.when(now)(functools.partial(what, s))
        return 0

    lax.fori_loop(0, len(steps), one_step, 0)

    for cp in last_copies(3):
        cp.wait_send()
    for s in range(4):
        for xx in range(4):
            result_copy(s, xx).wait()


def body(amplitudes, integrals, pair_energy, block_len):
    bf = lambda *shape: pltpu.VMEM(shape, BF)
    f32 = lambda *shape: pltpu.VMEM(shape, F32)
    dma = lambda *shape: pltpu.SemaphoreType.DMA(shape)
    scratch = [
        bf(4, 288, 576), bf(4, 288, 576),
        bf(4, 4, 1296, 128), bf(4, 4, 1296, 128),
        bf(1152, 768), bf(128, 512), bf(64, 128), bf(2, 384, 768),
        bf(4, 4, 144, 1152), bf(4, 4, 144, 1152), f32(4, 144, 1152),
        bf(4, 144, 1152), bf(4, 2, 144, 1152), bf(4, 144, 1152), bf(4, 2, 144, 1152),
        f32(4, 144, 1152), bf(4, 144, 1152), bf(4, 4, 336, 128),
        bf(4, 4, 336, 128), bf(4, 4, 336, 128), bf(4, 4, 336, 128),
        bf(512, 384), bf(192, 384), bf(4, 8, 176, 128), bf(4, 8, 176, 128), f32(2, 36, 4608),
        bf(288, 288), bf(128, 128), bf(128, 512), bf(64, 64),
        bf(256, 384), bf(4, 128, 384), bf(2, 128, 384),
        bf(2048, 1152), bf(16, 1024), f32(4, 40, 128), f32(4, 36, 4608),
        dma(4, 2), dma(4, 2, 2, 2), dma(4, 2, 2, 2), dma(4, 2, 2), dma(4, 2, 2), dma(4, 3, 4), dma(4, 3, 4),
        dma(4, 3, 2), dma(4, 3, 2), dma(4, 3, 2), dma(4, 3, 2),
        dma(4, 3), dma(4, 3), dma(4, 3, 2), dma(4, 3, 2), dma(4, 7), dma(4, 7), dma(4, 4),
    ]
    count, npairs = pair_energy.shape
    turned = pl.pallas_call(
        kernel,
        out_shape=pltpu.VMEM((npairs // 128, count, npairs), F32),
        in_specs=[
            pl.BlockSpec(memory_space=pl.ANY),
            pl.BlockSpec(memory_space=pl.ANY),
            pl.BlockSpec(memory_space=pltpu.VMEM),
            pl.BlockSpec(memory_space=pltpu.SMEM),
        ],
        out_specs=pl.BlockSpec(memory_space=pltpu.VMEM),
        scratch_shapes=scratch,
        compiler_params=pltpu.CompilerParams(
            collective_id=0, has_side_effects=True, vmem_limit_bytes=121 << 19
        ),
        name="cycle",
    )(amplitudes, jnp.swapaxes(integrals, 1, 2), pair_energy, block_len)
    return jnp.swapaxes(turned, 0, 1)


def solution(mesh):
    return jax.shard_map(
        body,
        mesh=mesh,
        in_specs=(P(None, "row", "col"), P(None, "col", "row"), P(), P()),
        out_specs=P(None, ("row", "col"), None),
        check_vma=False,
    )
```
